768 devices in a mesh: store: 64 (over y, x, core), grp: 12 (over z).
Axes of the slice: x: 4, y: 8, z: 12, core: 2. Of those that a mesh axis runs over, the one named last changes fastest.
Arguments:
- layer_input: bfloat16 [12, 64, 128, 1024], P('grp', 'store'), may hold values from -6 to 6
- initial: bfloat16 [12, 64, 128, 1024], P('grp', 'store'), may hold values from -6 to 6
- history: bfloat16 [2, 12, 8192, 1024], P(None, 'grp', 'store'), may hold values from -6 to 6
- batch_ids: int32 [12, 64, 64, 2], P('grp', 'store'), may hold values from 0 to 127, as said below
- batch_count: int32 [12, 64, 64], P('grp', 'store'), may hold values from 1 to 2, as said below
- halo_ids: int32 [12, 64, 64, 2], P('grp', 'store'), may hold values from 0 to 127, as said below
- halo_count: int32 [12, 64, 64], P('grp', 'store'), may hold values from 1 to 2, as said below
- block_cols: int32 [12, 64, 2, 4], P('grp', 'store'), may hold values from 0 to 3, all different within a row
- block_vals: bfloat16 [12, 64, 2, 4, 64, 64], P('grp', 'store'), may hold values from -0.375 to 0.375
- weight_one: bfloat16 [1024, 1024], replicated, may hold values from -0.1875 to 0.1875
- weight_two: bfloat16 [1024, 1024], replicated, may hold values from -0.1875 to 0.1875
- cotangent: bfloat16 [12, 64, 128, 1024], P('grp', 'store'), may hold values from -6 to 6
Outputs:
- new_history: bfloat16 [2, 12, 8192, 1024], P(None, 'grp', 'store')
- grad_two: float32 [1024, 1024], P('store')
The draws below stay inside these ranges and needn't reach their ends.
Inputs may be any that keep to these rules, and one draw needn't show every extreme that they name: `batch_ids`: within one group the batch slots of all devices name each owner's rows at most once. `batch_count`: in each group one owner has all 2 slots live from every device. `halo_ids`: the rows one device names of one owner are distinct. `halo_count`: in each group one owner has all 2 slots live from every device.
All inputs are finite; a program needn't handle non-finite values.
Results may differ from the reference program's by a relative error of at most 0.0054.
Values may be sent and summed in bfloat16 or wider, within the bound.
A program may use at most 64 MiB of HBM per device.

```python
import math
import jax
import jax.numpy as jnp
from jax import lax

H = 1024
BROWS = 128
BLK = 64
KB = 4
PCAP = 2
CAP = 2
NB = 2
NCB = 4
N_STORE = 64
N_GRP = 12


def draw_batch_ids(key, part):
    key = jax.random.fold_in(key, 11)
    ranks = jnp.broadcast_to(jnp.arange(BROWS, dtype=jnp.int32), (N_GRP, N_STORE, BROWS))
    shuffled = jax.random.permutation(key, ranks, axis=2, independent=True)
    chosen = shuffled.reshape(N_GRP, N_STORE, N_STORE, PCAP)
    return jnp.transpose(chosen, (0, 2, 1, 3))


def ragged_counts(key, top_count):
    first, second = jax.random.split(key)
    counts = jax.random.randint(first, (N_GRP, N_STORE, N_STORE), 1, top_count + 1, dtype=jnp.int32)
    busiest = jax.random.randint(second, (N_GRP, 1, 1), 0, N_STORE, dtype=jnp.int32)
    owner_index = jnp.arange(N_STORE, dtype=jnp.int32)[None, None, :]
    return jnp.where(owner_index == busiest, top_count, counts).astype(jnp.int32)


def draw_batch_count(key, part):
    key = jax.random.fold_in(key, 12)
    return ragged_counts(key, PCAP)


def draw_halo_ids(key, part):
    key = jax.random.fold_in(key, 13)
    ranks = jnp.broadcast_to(jnp.arange(BROWS, dtype=jnp.int32), (N_GRP, N_STORE, N_STORE, BROWS))
    shuffled = jax.random.permutation(key, ranks, axis=3, independent=True)
    return shuffled[:, :, :, :CAP]


def draw_halo_count(key, part):
    key = jax.random.fold_in(key, 14)
    return ragged_counts(key, CAP)


def steps_of(stream_key, extent, cuts, least, high):
    gain, own = 1.0, jax.random.fold_in(stream_key, 6)
    for position, blocks in cuts:
        heights = jnp.exp(jax.random.uniform(jax.random.fold_in(own, position), (blocks,), jnp.float32, least / len(cuts), high / len(cuts)))
        gain = gain * jnp.repeat(heights, extent[position] // blocks).reshape([-1 if axis == position else 1 for axis in range(len(extent))])
    return gain


def different_ones(own_key, rows, count, top, lift):
    sequence = jax.random.permutation(jax.random.fold_in(own_key, 1), count)
    favour = sequence
    for power in range(3):
        favour = favour * favour // count
    favour = favour * lift // count
    tickets = jax.random.randint(jax.random.fold_in(own_key, 2), (rows, count), 0, 4096) + favour
    sure = jax.random.permutation(jax.random.fold_in(own_key, 3), rows)[jnp.arange(count) % rows]
    tickets = jnp.where(jnp.arange(rows)[:, None] == sure[None, :], 1 << 14, tickets)
    priority = tickets * count + jnp.arange(count)
    return lax.top_k(priority.astype(jnp.int32), top)[1].astype(jnp.int32)


def scatter_about(own_key, extent, width, reach, shards=(), kind=jnp.bfloat16):
    drawn = width * jax.random.normal(own_key, extent, jnp.float32)
    if shards:
        drawn = drawn * steps_of(own_key, extent, shards, -0.22, 0.18)
    return jnp.clip(drawn, -reach, reach).astype(kind)


def setup_inputs(seed: int = 0) -> dict:
    key_of = jax.random.split(jax.random.key(seed), 13)
    layer_input = scatter_about(key_of[0], (N_GRP, N_STORE, BROWS, H), 1.0, 6.0, ((0, 12), (1, 64)))
    initial = scatter_about(key_of[1], (N_GRP, N_STORE, BROWS, H), 1.0, 6.0, ((0, 12), (1, 64)))
    history = scatter_about(key_of[2], (2, N_GRP, N_STORE * BROWS, H), 1.0, 6.0, ((1, 12), (2, 64)))
    batch_ids = draw_batch_ids(jax.random.fold_in(key_of[12], 71), 0)
    batch_count = draw_batch_count(jax.random.fold_in(key_of[12], 71), 0)
    halo_ids = draw_halo_ids(jax.random.fold_in(key_of[12], 71), 0)
    halo_count = draw_halo_count(jax.random.fold_in(key_of[12], 71), 0)
    block_cols = different_ones(key_of[7], N_GRP * N_STORE * NB, NCB, KB, 0).reshape((N_GRP, N_STORE, NB, KB))
    block_vals = scatter_about(key_of[8], (N_GRP, N_STORE, NB, KB, BLK, BLK), (KB * BLK) ** -0.5, 0.375, ((0, 12), (1, 64)))
    weight_one = scatter_about(key_of[9], (H, H), H ** -0.5, 0.1875)
    weight_two = scatter_about(key_of[10], (H, H), H ** -0.5, 0.1875)
    cotangent = scatter_about(key_of[11], (N_GRP, N_STORE, BROWS, H), 1.0, 6.0, ((0, 12), (1, 64)))
    return {"layer_input": layer_input, "initial": initial, "history": history, "batch_ids": batch_ids, "batch_count": batch_count, "halo_ids": halo_ids, "halo_count": halo_count, "block_cols": block_cols, "block_vals": block_vals, "weight_one": weight_one, "weight_two": weight_two, "cotangent": cotangent}


ALPHA = 0.1
BETA_ONE = math.log(1.5)
BETA_TWO = math.log(1.25)

def live_mask(counts, slots_per):
    slot_index = jnp.arange(slots_per, dtype=jnp.int32)[None, :]
    return (slot_index < counts[:, None]).reshape(-1)

def spread(col_blocks, block_values, fresh):
    blocks = fresh.reshape(-1, block_values.shape[2], fresh.shape[1])
    picked = blocks[col_blocks]
    aggregate = jnp.einsum('rkij,rkjh->rih', block_values.astype(jnp.float32), picked.astype(jnp.float32))
    return aggregate.reshape(-1, fresh.shape[1])

def gcn_layer(layer_rows, pulled, batch_live, halo_live, initial, col_blocks, block_values, weight, mixing):
    fresh = jnp.concatenate([jnp.where(batch_live[:, None], layer_rows, jnp.zeros_like(layer_rows)), jnp.where(halo_live[:, None], pulled, jnp.zeros_like(pulled))], axis=0)
    aggregate = spread(col_blocks, block_values, fresh)
    support = ((1.0 - ALPHA) * aggregate + ALPHA * initial.astype(jnp.float32)).astype(jnp.bfloat16)
    preact = (1.0 - mixing) * support.astype(jnp.float32) + mixing * jnp.dot(support, weight, preferred_element_type=jnp.float32)
    return (support, preact)

def gelu_tanh(pre_act):
    return jax.nn.gelu(pre_act, approximate=True)

def reference(layer_input, initial, history, batch_ids, batch_count, halo_ids, halo_count, block_cols, block_vals, weight_one, weight_two, cotangent):
    groups = N_GRP
    store_count = N_STORE

    def flatten(array):
        return array.reshape((groups * store_count,) + array.shape[2:])
    device_index = jnp.arange(groups * store_count, dtype=jnp.int32)
    owners = jnp.arange(store_count, dtype=jnp.int32)[:, None] * BROWS

    def device_step(running, pieces):
        which, rows_in, first_rows, b_cnt, h_wanted, h_cnt, col_blocks, block_values, cotan_rows = pieces
        group_history = lax.dynamic_index_in_dim(history, which // store_count, axis=1, keepdims=False)
        pulled = jnp.take(group_history, (owners + h_wanted).reshape(-1), axis=1)
        batch_live = live_mask(b_cnt, PCAP)
        halo_live = live_mask(h_cnt, CAP)
        support_one, preact_one = gcn_layer(rows_in, pulled[0], batch_live, halo_live, first_rows, col_blocks, block_values, weight_one, BETA_ONE)
        fresh_one = gelu_tanh(preact_one).astype(jnp.bfloat16)
        support_two, preact_two = gcn_layer(fresh_one, pulled[1], batch_live, halo_live, first_rows, col_blocks, block_values, weight_two, BETA_TWO)
        unused, pull_back = jax.vjp(gelu_tanh, preact_two)
        grad_pre = jnp.where(batch_live[:, None], pull_back(cotan_rows.astype(jnp.float32))[0], 0.0).astype(jnp.bfloat16)
        outer = lax.dot_general(support_two, grad_pre, (((0,), (0,)), ((), ())), preferred_element_type=jnp.float32)
        return (running + outer, fresh_one)
    gradient, fresh_all = lax.scan(device_step, jnp.zeros((H, H), jnp.float32), (device_index, flatten(layer_input), flatten(initial), flatten(batch_count), flatten(halo_ids), flatten(halo_count), flatten(block_cols), flatten(block_vals), flatten(cotangent)))
    gradient = gradient * (BETA_TWO / math.sqrt(groups * store_count * BROWS))
    slot_index = jnp.arange(PCAP, dtype=jnp.int32)[None, None, None, :]
    live_slots = slot_index < batch_count[:, :, :, None]
    owner_base = jnp.arange(store_count, dtype=jnp.int32)[None, None, :, None] * BROWS
    targets = jnp.where(live_slots, owner_base + batch_ids, store_count * BROWS).astype(jnp.int32)
    group_index = jnp.arange(groups, dtype=jnp.int32)[:, None, None, None]
    shaped_in = layer_input.reshape(groups, store_count, store_count, PCAP, H)
    shaped_fresh = fresh_all.reshape(groups, store_count, store_count, PCAP, H)
    history_zero = history[0].at[group_index, targets].set(shaped_in, mode='drop')
    history_one = history[1].at[group_index, targets].set(shaped_fresh, mode='drop')
    return (jnp.stack([history_zero, history_one]), gradient)
```

```python
import functools
import math

import jax
import jax.numpy as jnp
from jax import lax
from jax.experimental import pallas as pl
from jax.experimental.pallas import tpu as pltpu
from jax.sharding import PartitionSpec as P

ALPHA = 0.1
BETA_ONE = math.log(1.5)
BETA_TWO = math.log(1.25)
GELU_K = math.sqrt(2.0 / math.pi)
GELU_C = 0.044715
MESH = pl.DeviceIdType.MESH
NX = 4
CW = 256
PW = 128
VMEM_BYTES = 63 << 20
F32 = jnp.float32
BF = jnp.bfloat16
I32 = jnp.int32


def kernel(
    dims,
    x_hbm,
    init_hbm,
    hist_hbm,
    bid_hbm,
    bcnt_hbm,
    hid_hbm,
    hcnt_hbm,
    cols_hbm,
    vals_hbm,
    w1_hbm,
    w2_hbm,
    cot_hbm,
    newhist,
    grad,
    x_v,
    init_v,
    hist_v,
    bid_v,
    bcnt_v,
    hid_v,
    hcnt_v,
    cols_v,
    vals_v,
    w1_v,
    w2_v,
    cot_v,
    id_s,
    id_r,
    stage_a,
    stage_b,
    stage_c,
    halo_s0,
    halo_s1,
    halo_r0,
    halo_r1,
    push_s0,
    push_s1,
    push_r0,
    push_r1,
    adj,
    rows1,
    rows2,
    sup,
    sup_c,
    s_full,
    g_full,
    xs,
    xr,
    ys,
    yr,
    zs,
    zr,
    zo,
    lsem,
    id_sem,
    halo_sem,
    push_sem,
    core_sem,
    x_ssem,
    x_rsem,
    y_ssem,
    y_rsem,
    z_sem,
):
    ns, nz, ny, nx, h, j = dims
    cb = h // 128
    nr = 2 * ns
    nch = h // CW
    npiece = h // PW
    me = lax.axis_index("store")
    z = lax.axis_index("grp")
    core = me % 2
    my_x = (me // 2) % nx
    my_y = me // (2 * nx)

    def device(y, x, c):
        return {"store": (y * nx + x) * 2 + c}

    locals_ = [
        (hid_hbm.at[0, 0], hid_v),
        (bid_hbm.at[0, 0], bid_v),
        (bcnt_hbm.at[0], bcnt_v),
        (hcnt_hbm.at[0], hcnt_v),
        (cols_hbm.at[0, 0], cols_v),
        (vals_hbm.at[0, 0], vals_v),
        (x_hbm.at[0, 0], x_v),
        (hist_hbm.at[:, 0], hist_v),
        (init_hbm.at[0, 0], init_v),
        (w1_hbm, w1_v),
        (w2_hbm, w2_v),
        (cot_hbm.at[0, 0], cot_v),
    ]
    loads = [pltpu.make_async_copy(a, b, lsem.at[i]) for i, (a, b) in enumerate(locals_)]
    for load in loads:
        load.start()

    barrier = pltpu.get_barrier_semaphore()

    def greet_store(i, carry):
        pl.semaphore_signal(barrier, inc=1, device_id={"store": (me + i) % ns}, device_id_type=MESH)
        return carry

    def greet_grp(i, carry):
        pl.semaphore_signal(barrier, inc=1, device_id={"grp": (z + i) % nz}, device_id_type=MESH)
        return carry

    lax.fori_loop(1, ns, greet_store, 0)
    lax.fori_loop(1, nz, greet_grp, 0)

    for i in range(6):
        loads[i].wait()
    lane_s = lax.broadcasted_iota(I32, (ns, 128), 1)
    eye_o = lax.broadcasted_iota(I32, (ns, ns), 0) == lax.broadcasted_iota(I32, (ns, ns), 1)

    def column(row):
        spread = jnp.broadcast_to(row.astype(F32), (ns, ns))
        return jnp.sum(jnp.where(eye_o, spread, 0.0), axis=1, keepdims=True)

    count_row = bcnt_v[...]
    entries = [column(hid_v[c : c + 1, :]) for c in range(2)]
    entries += [column(jnp.where(count_row > c, bid_v[c : c + 1, :], nr)) for c in range(2)]
    message = entries[3]
    for c in (2, 1, 0):
        message = jnp.where(lane_s == c, entries[c], message)
    id_s[...] = message.astype(I32).reshape(ns, 1, 128)

    slot_row = lax.broadcasted_iota(I32, (nr, ns), 0)
    owner_lane = lax.broadcasted_iota(I32, (nr, ns), 1)
    of_owner = (slot_row >> 1) == owner_lane
    slot_c = (lax.broadcasted_iota(I32, (nr, 1), 0) & 1).astype(F32)

    def live(counts):
        spread = jnp.broadcast_to(counts[...].astype(F32), (nr, ns))
        count = jnp.sum(jnp.where(of_owner, spread, 0.0), axis=1, keepdims=True)
        return jnp.where(slot_c < count, 1.0, 0.0)

    live_b = live(bcnt_v)
    live_h = live(hcnt_v)

    blk = nr // 2
    for r in range(2):
        acc = jnp.zeros((blk, 4 * blk), F32)
        for k in range(4):
            lane = lax.broadcasted_iota(I32, (blk, 4 * blk), 1)
            row = lax.broadcasted_iota(I32, (blk, 4 * blk), 0)
            target = row + cols_v[r : r + 1, k : k + 1] * blk
            select = jnp.where(lane == target, 1.0, 0.0).astype(BF)
            acc += jnp.dot(vals_v[r, k], select, preferred_element_type=F32)
        adj[r * blk : (r + 1) * blk, :] = acc.astype(BF)

    def to_message(rows, stage, buffer):
        for b in range(cb):
            stage[pl.ds(b, nr, stride=cb), :] = rows[:, b * 128 : (b + 1) * 128].astype(F32)
        buffer[...] = stage[...].astype(BF).reshape(ns, 2 * cb, 128)

    loads[6].wait()
    to_message(x_v[...], stage_a, push_s0)
    rows1[0:nr, :] = (x_v[...].astype(F32) * live_b).astype(BF)
    loads[7].wait()

    pl.semaphore_wait(barrier, ns - 1 + nz - 1)

    def exchange(source, target, ssem, rsem):
        def send(i, carry):
            peer = (me + i) % ns
            pltpu.make_async_remote_copy(
                src_ref=source.at[peer],
                dst_ref=target.at[me],
                send_sem=ssem,
                recv_sem=rsem,
                device_id={"store": peer},
                device_id_type=MESH,
            ).start()
            return carry

        lax.fori_loop(1, ns, send, 0)

    def arrive(buffer, count, sem):
        part = buffer.at[pl.ds(0, count)]
        pltpu.make_async_copy(part, part, sem).wait()

    exchange(id_s, id_r, id_sem.at[0], id_sem.at[1])
    exchange(push_s0, push_r0, push_sem.at[0], push_sem.at[1])
    id_r[me] = id_s[me]
    push_r0[me] = push_s0[me]
    arrive(id_r, ns - 1, id_sem.at[1])

    asked = id_r[...].reshape(ns, 128)
    lane_r = lax.broadcasted_iota(I32, (ns, nr), 1)

    def hot(k):
        return jnp.where(asked[:, k : k + 1] == lane_r, 1.0, 0.0)

    wanted = jnp.concatenate([hot(0), hot(1)], axis=0).astype(BF)

    def gather(layer, stage, buffer):
        found = jnp.dot(wanted, hist_v[layer], preferred_element_type=F32)
        for c in range(2):
            for b in range(cb):
                stage[pl.ds(c * cb + b, ns, stride=2 * cb), :] = found[
                    c * ns : (c + 1) * ns, b * 128 : (b + 1) * 128
                ]
        buffer[...] = stage[...].astype(BF).reshape(ns, 2 * cb, 128)

    gather(0, stage_b, halo_s0)
    exchange(halo_s0, halo_r0, halo_sem.at[0], halo_sem.at[1])
    gather(1, stage_c, halo_s1)
    exchange(halo_s1, halo_r1, halo_sem.at[2], halo_sem.at[3])
    halo_r0[me] = halo_s0[me]
    halo_r1[me] = halo_s1[me]

    def land(buffer, stage, rows):
        stage[...] = buffer[...].reshape(nr * cb, 128).astype(F32)
        for b in range(cb):
            block = stage[pl.ds(b, nr, stride=cb), :] * live_h
            rows[nr : 2 * nr, b * 128 : (b + 1) * 128] = block.astype(BF)

    def support(rows):
        for n in range(nch):
            part = slice(n * CW, (n + 1) * CW)
            aggregate = jnp.dot(adj[...], rows[:, part], preferred_element_type=F32)
            mixed = (1.0 - ALPHA) * aggregate + ALPHA * init_v[:, part].astype(F32)
            sup[:, part] = mixed.astype(BF)

    def preact(weight, beta, n):
        part = slice(n * CW, (n + 1) * CW)
        product = jnp.dot(sup[...], weight[:, part], preferred_element_type=F32)
        return (1.0 - beta) * sup[:, part].astype(F32) + beta * product

    loads[8].wait()
    loads[9].wait()
    arrive(halo_r0, ns - 1, halo_sem.at[1])
    land(halo_r0, stage_b, rows1)
    support(rows1)
    for n in range(nch):
        part = slice(n * CW, (n + 1) * CW)
        pre = preact(w1_v, BETA_ONE, n)
        inner = jnp.tanh(GELU_K * (pre + GELU_C * (pre * pre * pre)))
        fresh = (0.5 * pre * (1.0 + inner)).astype(BF).astype(F32)
        rows2[0:nr, part] = (fresh * live_b).astype(BF)
        for b in range(CW // 128):
            stage_a[pl.ds(n * (CW // 128) + b, nr, stride=cb), :] = fresh[:, b * 128 : (b + 1) * 128]
    push_s1[...] = stage_a[...].astype(BF).reshape(ns, 2 * cb, 128)
    exchange(push_s1, push_r1, push_sem.at[2], push_sem.at[3])
    push_r1[me] = push_s1[me]

    loads[10].wait()
    loads[11].wait()
    arrive(halo_r1, ns - 1, halo_sem.at[3])
    land(halo_r1, stage_c, rows2)
    support(rows2)

    wide = 4 * nx * j
    half = wide // 2
    lane_to = lax.broadcasted_iota(I32, (wide, wide), 1)
    lane_from = lax.broadcasted_iota(I32, (wide, wide), 0)
    lg_j = j.bit_length() - 1
    lg_x = nx.bit_length() - 1
    from_j = lane_from & (j - 1)
    from_c = (lane_from >> lg_j) & 1
    from_x = (lane_from >> (lg_j + 1)) & (nx - 1)
    from_y = lane_from >> (lg_j + 1 + lg_x)
    goes = from_c * half + from_y * (nx * j) + from_x * j + from_j
    shuffle = jnp.where(goes == lane_to, 1.0, 0.0).astype(BF)
    for t in range(h // wide):
        moved = jnp.dot(sup[:, t * wide : (t + 1) * wide], shuffle, preferred_element_type=F32).astype(BF)
        sup_c[0, :, t * half : (t + 1) * half] = moved[:, :half]
        sup_c[1, :, t * half : (t + 1) * half] = moved[:, half:]
    partner = device(my_y, my_x, 1 - core)
    send_s = pltpu.make_async_remote_copy(
        src_ref=sup_c.at[1 - core],
        dst_ref=s_full.at[pl.ds(nr, nr)],
        send_sem=core_sem.at[0],
        recv_sem=core_sem.at[1],
        device_id=partner,
        device_id_type=MESH,
    )
    send_s.start()
    s_full[0:nr, :] = sup_c[core]
    for n in range(nch):
        part = slice(n * CW, (n + 1) * CW)
        pre = preact(w2_v, BETA_TWO, n)
        square = pre * pre
        inner = jnp.tanh(GELU_K * (pre + GELU_C * (square * pre)))
        slope = 0.5 * (1.0 + inner) + 0.5 * pre * (1.0 - inner * inner) * (
            GELU_K * (1.0 + 3.0 * GELU_C * square)
        )
        g_full[0:nr, part] = (live_b * (cot_v[:, part].astype(F32) * slope)).astype(BF)
    send_g = pltpu.make_async_remote_copy(
        src_ref=g_full.at[pl.ds(0, nr)],
        dst_ref=g_full.at[pl.ds(nr, nr)],
        send_sem=core_sem.at[2],
        recv_sem=core_sem.at[3],
        device_id=partner,
        device_id_type=MESH,
    )
    send_g.start()
    send_s.wait()
    send_g.wait()

    factor = BETA_TWO / math.sqrt(nz * ns * nr)
    for k in range(nch):
        share = factor * lax.dot_general(
            s_full[...],
            g_full[:, k * CW : (k + 1) * CW],
            (((0,), (0,)), ((), ())),
            preferred_element_type=F32,
        )
        for y in range(ny):
            for x in range(nx):
                at = (y * nx + x) * j
                xs[k, x, y * j : (y + 1) * j, :] = share[at : at + j, :].astype(BF)
        for i in range(1, nx):
            to_x = (my_x + i) % nx
            pltpu.make_async_remote_copy(
                src_ref=xs.at[k, to_x],
                dst_ref=xr.at[k, i - 1],
                send_sem=x_ssem.at[k],
                recv_sem=x_rsem.at[k],
                device_id=device(my_y, to_x, core),
                device_id_type=MESH,
            ).start()

    eye_r = lax.broadcasted_iota(I32, (nr, nr), 0) == lax.broadcasted_iota(I32, (nr, nr), 1)
    placed = jnp.concatenate([hot(2), hot(3)], axis=0)
    kept = jnp.where(eye_r, 1.0 - jnp.sum(placed, axis=0, keepdims=True), 0.0)
    place = jnp.concatenate([placed, kept], axis=0).astype(BF)

    def write_layer(layer, buffer, stage, rows):
        stage[...] = buffer[...].reshape(nr * cb, 128).astype(F32)
        for c in range(2):
            for b in range(cb):
                rows[c * ns : (c + 1) * ns, b * 128 : (b + 1) * 128] = stage[
                    pl.ds(c * cb + b, ns, stride=2 * cb), :
                ].astype(BF)
        rows[nr : 2 * nr, :] = hist_v[layer]
        newhist[layer, 0] = lax.dot_general(
            place, rows[...], (((0,), (0,)), ((), ())), preferred_element_type=F32
        ).astype(BF)

    arrive(push_r0, ns - 1, push_sem.at[1])
    write_layer(0, push_r0, stage_b, rows1)

    for k in range(nch):
        arrive(xr.at[k], nx - 1, x_rsem.at[k])
        total = xs[k, my_x].astype(F32)
        for i in range(nx - 1):
            total += xr[k, i].astype(F32)
        ys[k] = total.astype(BF).reshape(ny, j, CW)
        for i in range(1, ny):
            to_y = (my_y + i) % ny
            pltpu.make_async_remote_copy(
                src_ref=ys.at[k, to_y],
                dst_ref=yr.at[k, i - 1],
                send_sem=y_ssem.at[k],
                recv_sem=y_rsem.at[k],
                device_id=device(to_y, my_x, core),
                device_id_type=MESH,
            ).start()

    arrive(push_r1, ns - 1, push_sem.at[3])
    write_layer(1, push_r1, stage_c, rows2)

    per = CW // PW
    for k in range(nch):
        arrive(yr.at[k], ny - 1, y_rsem.at[k])
        total = ys[k, my_y].astype(F32)
        for i in range(ny - 1):
            total += yr[k, i].astype(F32)
        for p in range(per):
            piece = k * per + p
            goal = piece % nz
            zs[piece] = total[:, p * PW : (p + 1) * PW].astype(BF)

            @pl.when(z != goal)
            def _():
                pltpu.make_async_remote_copy(
                    src_ref=zs.at[piece],
                    dst_ref=zr.at[z],
                    send_sem=z_sem.at[0],
                    recv_sem=z_sem.at[1],
                    device_id={"grp": goal},
                    device_id_type=MESH,
                ).start()

            @pl.when(z == goal)
            def _():
                zr[z] = zs[piece]

    @pl.when(z < npiece)
    def _():
        arrive(zr, nz - 1, z_sem.at[1])
        total = zr[0].astype(F32)
        for i in range(1, nz):
            total += zr[i].astype(F32)
        zo[z] = total

        def send(i, carry):
            pltpu.make_async_remote_copy(
                src_ref=zo.at[z],
                dst_ref=zo.at[z],
                send_sem=z_sem.at[2],
                recv_sem=z_sem.at[3],
                device_id={"grp": (z + i) % nz},
                device_id_type=MESH,
            ).start()
            return carry

        lax.fori_loop(1, nz, send, 0)
        arrive(zo, npiece - 1, z_sem.at[3])

    @pl.when(z >= npiece)
    def _():
        arrive(zo, npiece, z_sem.at[3])

    for p in range(npiece):
        grad[:, p * PW : (p + 1) * PW] = zo[p]

    arrive(id_s, ns - 1, id_sem.at[0])
    arrive(push_s0, ns - 1, push_sem.at[0])
    arrive(push_s1, ns - 1, push_sem.at[2])
    arrive(halo_s0, ns - 1, halo_sem.at[0])
    arrive(halo_s1, ns - 1, halo_sem.at[2])
    for k in range(nch):
        arrive(xs.at[k], nx - 1, x_ssem.at[k])
        arrive(ys.at[k], ny - 1, y_ssem.at[k])

    @pl.when(z < npiece)
    def _():
        arrive(zs, npiece - 1, z_sem.at[0])
        arrive(zo, nz - 1, z_sem.at[2])

    @pl.when(z >= npiece)
    def _():
        arrive(zs, npiece, z_sem.at[0])


def per_device(*args):
    x, init, hist, bid, bcnt, hid, hcnt, cols, vals, w1, w2, cot = args
    ns, nz = lax.axis_size("store"), lax.axis_size("grp")
    h = x.shape[-1]
    nx = NX
    ny = ns // (2 * nx)
    j = h // ns
    nr = 2 * ns
    blk = nr // 2
    cb = h // 128
    nch = h // CW
    npiece = h // PW
    vm = pltpu.VMEM
    dma = pltpu.SemaphoreType.DMA
    slots = vm((ns, 2 * cb, 128), BF)
    stage = vm((nr * cb, 128), F32)
    scratch = [
        vm((nr, h), BF),
        vm((nr, h), BF),
        vm((2, nr, h), BF),
        vm((2, ns), I32),
        vm((1, ns), I32),
        vm((2, ns), I32),
        vm((1, ns), I32),
        vm((2, 4), I32),
        vm((2, 4, blk, blk), BF),
        vm((h, h), BF),
        vm((h, h), BF),
        vm((nr, h), BF),
        vm((ns, 1, 128), I32),
        vm((ns, 1, 128), I32),
        stage,
        stage,
        stage,
        slots,
        slots,
        slots,
        slots,
        slots,
        slots,
        slots,
        slots,
        vm((nr, 2 * nr), BF),
        vm((2 * nr, h), BF),
        vm((2 * nr, h), BF),
        vm((nr, h), BF),
        vm((2, nr, h // 2), BF),
        vm((2 * nr, h // 2), BF),
        vm((2 * nr, h), BF),
        vm((nch, nx, ny * j, CW), BF),
        vm((nch, nx - 1, ny * j, CW), BF),
        vm((nch, ny, j, CW), BF),
        vm((nch, ny - 1, j, CW), BF),
        vm((npiece, j, PW), BF),
        vm((nz, j, PW), BF),
        vm((nz, j, PW), F32),
        dma((12,)),
        dma((2,)),
        dma((4,)),
        dma((4,)),
        dma((4,)),
        dma((nch,)),
        dma((nch,)),
        dma((nch,)),
        dma((nch,)),
        dma((4,)),
    ]
    return pl.pallas_call(
        functools.partial(kernel, (ns, nz, ny, nx, h, j)),
        out_shape=(
            jax.ShapeDtypeStruct((2, 1, nr, h), BF),
            jax.ShapeDtypeStruct((j, h), F32),
        ),
        in_specs=[pl.BlockSpec(memory_space=pl.ANY)] * 12,
        out_specs=(
            pl.BlockSpec(memory_space=pltpu.VMEM),
            pl.BlockSpec(memory_space=pltpu.VMEM),
        ),
        scratch_shapes=scratch,
        compiler_params=pltpu.CompilerParams(
            collective_id=0, has_side_effects=True, vmem_limit_bytes=VMEM_BYTES
        ),
        name="gcnii",
    )(
        x,
        init,
        hist,
        jnp.swapaxes(bid, 2, 3),
        bcnt,
        jnp.swapaxes(hid, 2, 3),
        hcnt,
        cols,
        vals,
        w1,
        w2,
        cot,
    )


def solution(mesh):
    in_specs = (
        P("grp", "store", None, None),
        P("grp", "store", None, None),
        P(None, "grp", "store", None),
        P("grp", "store", None, None),
        P("grp", "store", None),
        P("grp", "store", None, None),
        P("grp", "store", None),
        P("grp", "store", None, None),
        P("grp", "store", None, None, None, None),
        P(),
        P(),
        P("grp", "store", None, None),
    )
    out_specs = (P(None, "grp", "store", None), P("store", None))
    return jax.shard_map(
        per_device, mesh=mesh, in_specs=in_specs, out_specs=out_specs, check_vma=False
    )
```

```python
import functools
import math

import jax
import jax.numpy as jnp
from jax import lax
from jax.experimental import pallas as pl
from jax.experimental.pallas import tpu as pltpu
from jax.sharding import PartitionSpec as P

ALPHA = 0.1
BETA_ONE = math.log(1.5)
BETA_TWO = math.log(1.25)
GELU_K = math.sqrt(2.0 / math.pi)
GELU_C = 0.044715
MESH = pl.DeviceIdType.MESH
NX = 4
WIDTHS = (256, 256, 256, 256)
PATHS = "xxxx"
FAR_FIRST = 1
CW = 256
FAR = {8: (3, 6), 2: (1, 2)}
PUSH0 = 3
NEAR1 = 0
VMEM_BYTES = 63 << 20
F32 = jnp.float32
BF = jnp.bfloat16
I32 = jnp.int32


def kernel(
    dims,
    x_hbm,
    init_hbm,
    hist_hbm,
    bid_hbm,
    bcnt_hbm,
    hid_hbm,
    hcnt_hbm,
    cols_hbm,
    vals_hbm,
    w1_hbm,
    w2_hbm,
    cot_hbm,
    newhist,
    grad,
    x_v,
    init_v,
    hist_v,
    bid_v,
    bcnt_v,
    hid_v,
    hcnt_v,
    cols_v,
    vals_v,
    w1_v,
    w2_v,
    cot_v,
    id_s,
    id_r,
    stage_a,
    stage_b,
    stage_c,
    halo_s0,
    halo_s1,
    halo_r0,
    halo_r1,
    push_s0,
    push_s1,
    push_r0,
    push_r1,
    adj,
    rows1,
    rows2,
    sup,
    sup_c,
    s_pair,
    hist_o,
    lsem,
    id_sem,
    halo_sem,
    push_sem,
    core_sem,
    x_ssem,
    x_rsem,
    y_ssem,
    y_rsem,
    z_ssem,
    z_rsem,
    osem,
    *chunks,
):
    ns, nz, ny, nx, h, j = dims
    cb = h // 128
    nr = 2 * ns
    nch = len(WIDTHS)
    starts = [sum(WIDTHS[:k]) for k in range(nch)]
    g_pair, xs, xr, ys, yr, zr = (chunks[i * nch : (i + 1) * nch] for i in range(6))
    w = 2 * nx
    far_lo, far_hi = (d * w for d in FAR[ny])
    near = [(1, far_lo), (far_hi, ns)]
    far = [(far_lo, far_hi)]
    me = lax.axis_index("store")
    z = lax.axis_index("grp")
    core = me % 2
    my_x = (me // 2) % nx
    my_y = me // w
    my_w = me % w

    def device(y, x, c):
        return {"store": (y * nx + x) * 2 + c}

    locals_ = [
        (hid_hbm.at[0, 0], hid_v),
        (bid_hbm.at[0, 0], bid_v),
        (bcnt_hbm.at[0], bcnt_v),
        (hcnt_hbm.at[0], hcnt_v),
        (cols_hbm.at[0, 0], cols_v),
        (vals_hbm.at[0, 0], vals_v),
        (x_hbm.at[0, 0], x_v),
        (hist_hbm.at[:, 0], hist_v),
        (init_hbm.at[0, 0], init_v),
        (w1_hbm, w1_v),
        (w2_hbm, w2_v),
        (cot_hbm.at[0, 0], cot_v),
    ]
    loads = [pltpu.make_async_copy(a, b, lsem.at[i]) for i, (a, b) in enumerate(locals_)]
    owed = {}
    for i, load in enumerate(loads):
        load.start()
        owed["load", i] = load.wait

    def settle(*name):
        owed.pop(name)()

    def finish():
        for name in list(owed):
            owed.pop(name)()

    barrier = pltpu.get_barrier_semaphore()

    def greet_store(i, carry):
        pl.semaphore_signal(barrier, inc=1, device_id={"store": (me + i) % ns}, device_id_type=MESH)
        return carry

    def greet_grp(i, carry):
        pl.semaphore_signal(barrier, inc=1, device_id={"grp": (z + i) % nz}, device_id_type=MESH)
        return carry

    lax.fori_loop(1, ns, greet_store, 0)
    lax.fori_loop(1, nz, greet_grp, 0)

    for i in range(3):
        settle("load", i)
    lane_s = lax.broadcasted_iota(I32, (ns, 128), 1)
    eye_o = lax.broadcasted_iota(I32, (ns, ns), 0) == lax.broadcasted_iota(I32, (ns, ns), 1)

    def column(row):
        spread = jnp.broadcast_to(row.astype(F32), (ns, ns))
        return jnp.sum(jnp.where(eye_o, spread, 0.0), axis=1, keepdims=True)

    count_row = bcnt_v[...]
    entries = [column(hid_v[c : c + 1, :]) for c in range(2)]
    entries += [column(jnp.where(count_row > c, bid_v[c : c + 1, :], nr)) for c in range(2)]
    message = entries[3]
    for c in (2, 1, 0):
        message = jnp.where(lane_s == c, entries[c], message)
    id_s[...] = message.astype(I32).reshape(ns, 1, 128)

    pl.semaphore_wait(barrier, ns - 1 + nz - 1)

    def arrive(buffer, count, sem):
        part = buffer.at[pl.ds(0, count)]
        pltpu.make_async_copy(part, part, sem).wait()

    def send_all(ranges, source, target, ssem, rsem, by_owner):
        def send(i, carry):
            along = i // w
            column = (my_w + i % w) % w
            peer = ((my_y + along) % ny) * w + column
            here = along * w + column
            there = ((ny - along) % ny) * w + my_w
            pltpu.make_async_remote_copy(
                src_ref=source.at[here if by_owner else peer],
                dst_ref=target.at[me if by_owner else there],
                send_sem=ssem,
                recv_sem=rsem,
                device_id={"store": peer},
                device_id_type=MESH,
            ).start()
            return carry

        for low, high in ranges:
            if low < high:
                lax.fori_loop(low, high, send, 0)
        return sum(high - low for low, high in ranges)

    def owe(name, buffer, count, sem):
        owed[name] = functools.partial(arrive, buffer, count, sem)

    def push(name, source, target, sems):
        count = send_all(near + far, source, target, sems.at[0], sems.at[1], False)
        owe((name, "out"), source, count, sems.at[0])
        owe((name, "in"), target, count, sems.at[1])

    for part, ranges in enumerate((far, near)):
        count = send_all(ranges, id_s, id_r, id_sem.at[part, 0], id_sem.at[part, 1], False)
        owe(("ids", "out", part), id_s, count, id_sem.at[part, 0])
        owe(("ids", "in", part), id_r, count, id_sem.at[part, 1])
    id_r[my_w] = id_s[me]

    for i in range(3, 6):
        settle("load", i)
    slot_row = lax.broadcasted_iota(I32, (nr, ns), 0)
    owner_lane = lax.broadcasted_iota(I32, (nr, ns), 1)
    of_owner = (slot_row >> 1) == owner_lane
    slot_c = (lax.broadcasted_iota(I32, (nr, 1), 0) & 1).astype(F32)

    def live(counts):
        spread = jnp.broadcast_to(counts[...].astype(F32), (nr, ns))
        count = jnp.sum(jnp.where(of_owner, spread, 0.0), axis=1, keepdims=True)
        return jnp.where(slot_c < count, 1.0, 0.0)

    live_b = live(bcnt_v)
    live_h = live(hcnt_v)

    blk = nr // 2
    for r in range(2):
        acc = jnp.zeros((blk, 4 * blk), F32)
        for k in range(4):
            lane = lax.broadcasted_iota(I32, (blk, 4 * blk), 1)
            row = lax.broadcasted_iota(I32, (blk, 4 * blk), 0)
            target = row + cols_v[r : r + 1, k : k + 1] * blk
            select = jnp.where(lane == target, 1.0, 0.0).astype(BF)
            acc += jnp.dot(vals_v[r, k], select, preferred_element_type=F32)
        adj[r * blk : (r + 1) * blk, :] = acc.astype(BF)

    def to_message(rows, stage, buffer):
        for b in range(cb):
            stage[pl.ds(b, nr, stride=cb), :] = rows[:, b * 128 : (b + 1) * 128].astype(F32)
        buffer[...] = stage[...].astype(BF).reshape(ns, 2 * cb, 128)

    settle("load", 6)
    rows1[0:nr, :] = (x_v[...].astype(F32) * live_b).astype(BF)
    to_message(rows1[0:nr, :], stage_a, push_s0)
    if PUSH0 == 3:
        push("push0", push_s0, push_r0, push_sem.at[0])
    push_r0[my_w] = push_s0[me]
    settle("load", 7)
    def hot(k, low, high):
        asked = id_r[low:high].reshape(high - low, 128)
        lane_r = lax.broadcasted_iota(I32, (high - low, nr), 1)
        return jnp.where(asked[:, k : k + 1] == lane_r, 1.0, 0.0)

    def gather(layer, ranges, stage, buffer):
        for low, high in ranges:
            size = high - low
            if size == 0:
                continue
            wanted = jnp.concatenate([hot(0, low, high), hot(1, low, high)], axis=0).astype(BF)
            found = jnp.dot(wanted, hist_v[layer], preferred_element_type=F32)
            for c in range(2):
                for b in range(cb):
                    stage[pl.ds(low * 2 * cb + c * cb + b, size, stride=2 * cb), :] = found[
                        c * size : (c + 1) * size, b * 128 : (b + 1) * 128
                    ]
            rows = stage[low * 2 * cb : high * 2 * cb, :]
            buffer[low:high] = rows.astype(BF).reshape(size, 2 * cb, 128)

    def reply(layer, ranges, source, target, sems, part):
        count = send_all(ranges, source, target, sems.at[part], sems.at[2], True)
        owe(("reply", layer, part), source, count, sems.at[part])

    near_rows = [(0, far_lo), (far_hi, ns)]
    settle("ids", "in", 1)
    gather(0, near_rows, stage_b, halo_s0)
    reply(0, near, halo_s0, halo_r0, halo_sem.at[0], 0)
    if NEAR1 == 1:
        gather(1, near_rows, stage_c, halo_s1)
        reply(1, near, halo_s1, halo_r1, halo_sem.at[1], 0)
    settle("ids", "in", 0)
    gather(0, far, stage_b, halo_s0)
    reply(0, far, halo_s0, halo_r0, halo_sem.at[0], 1)
    gather(1, far, stage_c, halo_s1)
    reply(1, far, halo_s1, halo_r1, halo_sem.at[1], 1)
    if NEAR1 == 0:
        gather(1, near_rows, stage_c, halo_s1)
        reply(1, near, halo_s1, halo_r1, halo_sem.at[1], 0)
    owe(("halo0", "in"), halo_r0, ns - 1, halo_sem.at[0, 2])
    owe(("halo1", "in"), halo_r1, ns - 1, halo_sem.at[1, 2])
    if PUSH0 == 0:
        push("push0", push_s0, push_r0, push_sem.at[0])
    halo_r0[me] = halo_s0[my_w]
    halo_r1[me] = halo_s1[my_w]

    def land(buffer, stage, rows):
        stage[...] = buffer[...].reshape(nr * cb, 128).astype(F32)
        for b in range(cb):
            block = stage[pl.ds(b, nr, stride=cb), :] * live_h
            rows[nr : 2 * nr, b * 128 : (b + 1) * 128] = block.astype(BF)

    def support(rows):
        for n in range(h // CW):
            part = slice(n * CW, (n + 1) * CW)
            aggregate = jnp.dot(adj[...], rows[:, part], preferred_element_type=F32)
            mixed = (1.0 - ALPHA) * aggregate + ALPHA * init_v[:, part].astype(F32)
            sup[:, part] = mixed.astype(BF)

    def preact(weight, beta, part):
        product = jnp.dot(sup[...], weight[:, part], preferred_element_type=F32)
        return (1.0 - beta) * sup[:, part].astype(F32) + beta * product

    settle("load", 8)
    settle("load", 9)
    settle("halo0", "in")
    land(halo_r0, stage_b, rows1)
    support(rows1)
    for n in range(h // CW):
        part = slice(n * CW, (n + 1) * CW)
        pre = preact(w1_v, BETA_ONE, part)
        inner = jnp.tanh(GELU_K * (pre + GELU_C * (pre * pre * pre)))
        fresh = (0.5 * pre * (1.0 + inner)).astype(BF).astype(F32)
        rows2[0:nr, part] = (fresh * live_b).astype(BF)
    to_message(rows2[0:nr, :], stage_a, push_s1)
    push("push1", push_s1, push_r1, push_sem.at[1])
    push_r1[my_w] = push_s1[me]
    if PUSH0 == 1:
        push("push0", push_s0, push_r0, push_sem.at[0])

    settle("load", 10)
    settle("load", 11)
    settle("halo1", "in")
    land(halo_r1, stage_c, rows2)
    support(rows2)

    wide = 4 * nx * j
    half = wide // 2
    lane_from = lax.broadcasted_iota(I32, (wide, wide), 1)
    row_to = lax.broadcasted_iota(I32, (wide, wide), 0)
    lg_j = j.bit_length() - 1
    lg_x = nx.bit_length() - 1
    from_j = lane_from & (j - 1)
    from_c = (lane_from >> lg_j) & 1
    from_x = (lane_from >> (lg_j + 1)) & (nx - 1)
    from_y = lane_from >> (lg_j + 1 + lg_x)
    goes = from_c * half + from_y * (nx * j) + from_x * j + from_j
    shuffle = jnp.where(goes == row_to, 1.0, 0.0).astype(BF)
    for t in range(h // wide):
        moved = lax.dot_general(
            shuffle,
            sup[:, t * wide : (t + 1) * wide],
            (((1,), (1,)), ((), ())),
            preferred_element_type=F32,
        ).astype(BF)
        sup_c[0, t * half : (t + 1) * half, :] = moved[:half]
        sup_c[1, t * half : (t + 1) * half, :] = moved[half:]
    partner = device(my_y, my_x, 1 - core)

    def to_partner(name, source, target, ssem, rsem):
        copy = pltpu.make_async_remote_copy(
            src_ref=source,
            dst_ref=target,
            send_sem=ssem,
            recv_sem=rsem,
            device_id=partner,
            device_id_type=MESH,
        )
        copy.start()
        owed[name] = copy.wait

    to_partner(("core", "s"), sup_c.at[1 - core], s_pair.at[1], core_sem.at[nch, 0], core_sem.at[nch, 1])
    s_pair[0] = sup_c[core]

    factor = BETA_TWO / math.sqrt(nz * ns * nr)

    along_x = (nx, my_x, lambda to: device(my_y, to, core))
    along_y = (ny, my_y, lambda to: device(to, my_x, core))

    def steps(count):
        if FAR_FIRST:
            return sorted(range(1, count), key=lambda i: -min(i, count - i))
        return range(1, count)

    def spread(name, k, axis, source, target, ssem, rsem):
        count, mine, to_device = axis
        for i in steps(count):
            to = (mine + i) % count
            pltpu.make_async_remote_copy(
                src_ref=source.at[to],
                dst_ref=target.at[i - 1],
                send_sem=ssem,
                recv_sem=rsem,
                device_id=to_device(to),
                device_id_type=MESH,
            ).start()
        owe((name, "in", k), target, count - 1, rsem)
        owe((name, "out", k), source, count - 1, ssem)

    def summed(axis, source, target):
        total = source[axis[1]].astype(F32)
        for i in range(axis[0] - 1):
            total += target[i].astype(F32)
        return total

    for n in range(nch + 1):
        if n < nch:
            part = slice(starts[n], starts[n] + WIDTHS[n])
            pre = preact(w2_v, BETA_TWO, part)
            square = pre * pre
            inner = jnp.tanh(GELU_K * (pre + GELU_C * (square * pre)))
            slope = 0.5 * (1.0 + inner) + 0.5 * pre * (1.0 - inner * inner) * (
                GELU_K * (1.0 + 3.0 * GELU_C * square)
            )
            g_pair[n][0] = (live_b * (cot_v[:, part].astype(F32) * slope)).astype(BF)
            to_partner(("core", n), g_pair[n].at[0], g_pair[n].at[1], core_sem.at[n, 0], core_sem.at[n, 1])
        if n == 1:
            settle("core", "s")
        if n >= 1:
            k = n - 1
            settle("core", k)
            share = factor * jnp.dot(
                jnp.concatenate([s_pair[0], s_pair[1]], axis=1),
                g_pair[k][...].reshape(2 * nr, WIDTHS[k]),
                preferred_element_type=F32,
            )
            if PATHS[k] == "x":
                for y in range(ny):
                    for x in range(nx):
                        at = (y * nx + x) * j
                        xs[k][x, y * j : (y + 1) * j, :] = share[at : at + j, :].astype(BF)
            else:
                xs[k][...] = share.astype(BF).reshape(ny, nx * j, WIDTHS[k])
            first = along_x if PATHS[k] == "x" else along_y
            spread("x", k, first, xs[k], xr[k], x_ssem.at[k], x_rsem.at[k])

    for k in range(nch + 1):
        if k < nch:
            first, second = (along_x, along_y) if PATHS[k] == "x" else (along_y, along_x)
            settle("x", "in", k)
            total = summed(first, xs[k], xr[k])
            ys[k][...] = total.astype(BF).reshape(second[0], j, WIDTHS[k])
            spread("y", k, second, ys[k], yr[k], y_ssem.at[k], y_rsem.at[k])
        if k >= 1:
            second = along_y if PATHS[k - 1] == "x" else along_x
            settle("y", "in", k - 1)
            total = summed(second, ys[k - 1], yr[k - 1])
            zr[k - 1][z] = total.astype(BF)
            for i in steps(nz):
                pltpu.make_async_remote_copy(
                    src_ref=zr[k - 1].at[z],
                    dst_ref=zr[k - 1].at[z],
                    send_sem=z_ssem.at[k - 1],
                    recv_sem=z_rsem.at[k - 1],
                    device_id={"grp": (z + i) % nz},
                    device_id_type=MESH,
                ).start()
            owed["z", "in", k - 1] = functools.partial(arrive, zr[k - 1], nz - 1, z_rsem.at[k - 1])
            owed["z", "out", k - 1] = functools.partial(arrive, zr[k - 1], nz - 1, z_ssem.at[k - 1])

    eye_r = lax.broadcasted_iota(I32, (nr, nr), 0) == lax.broadcasted_iota(I32, (nr, nr), 1)
    placed = jnp.concatenate([hot(2, 0, ns), hot(3, 0, ns)], axis=0)
    kept = jnp.where(eye_r, 1.0 - jnp.sum(placed, axis=0, keepdims=True), 0.0)
    place = jnp.concatenate([placed, kept], axis=0).astype(BF)

    def write_layer(layer, buffer, stage, rows):
        stage[...] = buffer[...].reshape(nr * cb, 128).astype(F32)
        for c in range(2):
            for b in range(cb):
                rows[c * ns : (c + 1) * ns, b * 128 : (b + 1) * 128] = stage[
                    pl.ds(c * cb + b, ns, stride=2 * cb), :
                ].astype(BF)
        rows[nr : 2 * nr, :] = hist_v[layer]
        hist_o[layer] = lax.dot_general(
            place, rows[...], (((0,), (0,)), ((), ())), preferred_element_type=F32
        ).astype(BF)
        store = pltpu.make_async_copy(hist_o.at[layer], newhist.at[layer, 0], osem.at[layer])
        store.start()
        owed["store", layer] = store.wait

    settle("push0", "in")
    write_layer(0, push_r0, stage_b, rows1)
    settle("push1", "in")
    write_layer(1, push_r1, stage_c, rows2)

    for k in range(nch):
        settle("z", "in", k)
        total = zr[k][0].astype(F32)
        for i in range(1, nz):
            total += zr[k][i].astype(F32)
        grad[:, starts[k] : starts[k] + WIDTHS[k]] = total
    finish()


def copy_kernel(a, b, a_out, b_out):
    a_out[...] = a[...]
    b_out[...] = b[...]


def per_device(*args):
    x, init, hist, bid, bcnt, hid, hcnt, cols, vals, w1, w2, cot = args
    ns, nz = lax.axis_size("store"), lax.axis_size("grp")
    h = x.shape[-1]
    nx = NX
    ny = ns // (2 * nx)
    j = h // ns
    nr = 2 * ns
    blk = nr // 2
    cb = h // 128
    nch = len(WIDTHS)
    vm = pltpu.VMEM
    dma = pltpu.SemaphoreType.DMA
    slots = vm((ns, 2 * cb, 128), BF)
    stage = vm((nr * cb, 128), F32)
    scratch = [
        vm((nr, h), BF),
        vm((nr, h), BF),
        vm((2, nr, h), BF),
        vm((2, ns), I32),
        vm((1, ns), I32),
        vm((2, ns), I32),
        vm((1, ns), I32),
        vm((2, 4), I32),
        vm((2, 4, blk, blk), BF),
        vm((h, h), BF),
        vm((h, h), BF),
        vm((nr, h), BF),
        vm((ns, 1, 128), I32),
        vm((ns, 1, 128), I32),
        stage,
        stage,
        stage,
        slots,
        slots,
        slots,
        slots,
        slots,
        slots,
        slots,
        slots,
        vm((nr, 2 * nr), BF),
        vm((2 * nr, h), BF),
        vm((2 * nr, h), BF),
        vm((nr, h), BF),
        vm((2, h // 2, nr), BF),
        vm((2, h // 2, nr), BF),
        vm((2, nr, h), BF),
        dma((12,)),
        dma((2, 2)),
        dma((2, 3)),
        dma((2, 2)),
        dma((nch + 1, 2)),
        dma((nch,)),
        dma((nch,)),
        dma((nch,)),
        dma((nch,)),
        dma((nch,)),
        dma((nch,)),
        dma((2,)),
    ]
    scratch += [vm((2, nr, c), BF) for c in WIDTHS]
    sizes = [(nx, ny, c) if p == "x" else (ny, nx, c) for p, c in zip(PATHS, WIDTHS)]
    scratch += [vm((a, b * j, c), BF) for a, b, c in sizes]
    scratch += [vm((a - 1, b * j, c), BF) for a, b, c in sizes]
    scratch += [vm((b, j, c), BF) for a, b, c in sizes]
    scratch += [vm((b - 1, j, c), BF) for a, b, c in sizes]
    scratch += [vm((nz, j, c), BF) for c in WIDTHS]
    results = pl.pallas_call(
        functools.partial(kernel, (ns, nz, ny, nx, h, j)),
        out_shape=(
            jax.ShapeDtypeStruct((2, 1, nr, h), BF),
            jax.ShapeDtypeStruct((j, h), F32),
        ),
        in_specs=[pl.BlockSpec(memory_space=pl.ANY)] * 12,
        out_specs=(
            pl.BlockSpec(memory_space=pl.ANY),
            pl.BlockSpec(memory_space=pltpu.VMEM),
        ),
        scratch_shapes=scratch,
        compiler_params=pltpu.CompilerParams(
            collective_id=0, has_side_effects=True, vmem_limit_bytes=VMEM_BYTES
        ),
        name="gcnii",
    )(
        x,
        init,
        hist,
        jnp.swapaxes(bid, 2, 3),
        bcnt,
        jnp.swapaxes(hid, 2, 3),
        hcnt,
        cols,
        vals,
        w1,
        w2,
        cot,
    )
    specs = (
        pl.BlockSpec((2, 1, nr // 2, h), lambda i: (0, 0, i, 0)),
        pl.BlockSpec((j, h // 2), lambda i: (0, i)),
    )
    return pl.pallas_call(
        copy_kernel,
        grid=(2,),
        out_shape=(
            jax.ShapeDtypeStruct((2, 1, nr, h), BF),
            jax.ShapeDtypeStruct((j, h), F32),
        ),
        in_specs=specs,
        out_specs=specs,
        compiler_params=pltpu.CompilerParams(vmem_limit_bytes=VMEM_BYTES),
        name="write_out",
    )(*results)


def solution(mesh):
    in_specs = (
        P("grp", "store", None, None),
        P("grp", "store", None, None),
        P(None, "grp", "store", None),
        P("grp", "store", None, None),
        P("grp", "store", None),
        P("grp", "store", None, None),
        P("grp", "store", None),
        P("grp", "store", None, None),
        P("grp", "store", None, None, None, None),
        P(),
        P(),
        P("grp", "store", None, None),
    )
    out_specs = (P(None, "grp", "store", None), P("store", None))
    return jax.shard_map(
        per_device, mesh=mesh, in_specs=in_specs, out_specs=out_specs, check_vma=False
    )
```

```python
import functools
import math

import jax
import jax.numpy as jnp
from jax import lax
from jax.experimental import pallas as pl
from jax.experimental.pallas import tpu as pltpu
from jax.sharding import PartitionSpec as P

ALPHA = 0.1
BETA_ONE = math.log(1.5)
BETA_TWO = math.log(1.25)
GELU_K = math.sqrt(2.0 / math.pi)
GELU_C = 0.044715
MESH = pl.DeviceIdType.MESH
NX = 4
WIDTHS = (256, 256, 256, 256)
PATHS = "xxxx"
FAR_FIRST = 1
CW = 256
FAR = {8: (3, 6), 2: (1, 2)}
PUSH0 = 3
NEAR1 = 0
VMEM_BYTES = 63 << 20
F32 = jnp.float32
BF = jnp.bfloat16
I32 = jnp.int32


def kernel(
    dims,
    x_hbm,
    init_hbm,
    hist_hbm,
    bid_hbm,
    bcnt_hbm,
    hid_hbm,
    hcnt_hbm,
    cols_hbm,
    vals_hbm,
    w1_hbm,
    w2_hbm,
    cot_hbm,
    newhist,
    grad,
    x_v,
    init_v,
    hist_v,
    bid_v,
    bcnt_v,
    hid_v,
    hcnt_v,
    cols_v,
    vals_v,
    w1_v,
    w2_v,
    cot_v,
    id_s,
    id_r,
    stage_a,
    stage_b,
    stage_c,
    halo_s0,
    halo_s1,
    halo_r0,
    halo_r1,
    push_s0,
    push_s1,
    push_r0,
    push_r1,
    adj,
    rows1,
    rows2,
    sup,
    sup_c,
    s_pair,
    hist_o,
    grad_v,
    lsem,
    id_sem,
    halo_sem,
    push_sem,
    core_sem,
    x_ssem,
    x_rsem,
    y_ssem,
    y_rsem,
    z_ssem,
    z_rsem,
    osem,
    *chunks,
):
    ns, nz, ny, nx, h, j = dims
    cb = h // 128
    nr = 2 * ns
    nch = len(WIDTHS)
    starts = [sum(WIDTHS[:k]) for k in range(nch)]
    g_pair, xs, xr, ys, yr, zr = (chunks[i * nch : (i + 1) * nch] for i in range(6))
    w = 2 * nx
    far_lo, far_hi = (d * w for d in FAR[ny])
    near = [(1, far_lo), (far_hi, ns)]
    far = [(far_lo, far_hi)]
    me = lax.axis_index("store")
    z = lax.axis_index("grp")
    core = me % 2
    my_x = (me // 2) % nx
    my_y = me // w
    my_w = me % w

    def device(y, x, c):
        return {"store": (y * nx + x) * 2 + c}

    locals_ = [
        (hid_hbm.at[0, 0], hid_v),
        (bid_hbm.at[0, 0], bid_v),
        (bcnt_hbm.at[0], bcnt_v),
        (hcnt_hbm.at[0], hcnt_v),
        (cols_hbm.at[0, 0], cols_v),
        (vals_hbm.at[0, 0], vals_v),
        (x_hbm.at[0, 0], x_v),
        (hist_hbm.at[:, 0], hist_v),
        (init_hbm.at[0, 0], init_v),
        (w1_hbm, w1_v),
        (w2_hbm, w2_v),
        (cot_hbm.at[0, 0], cot_v),
    ]
    loads = [pltpu.make_async_copy(a, b, lsem.at[i]) for i, (a, b) in enumerate(locals_)]
    owed = {}

    def begin(first, last):
        for i in range(first, last):
            loads[i].start()
            owed["load", i] = loads[i].wait

    begin(0, 3)

    def settle(*name):
        owed.pop(name)()

    def finish():
        for name in list(owed):
            owed.pop(name)()

    barrier = pltpu.get_barrier_semaphore()

    def greet_store(i, carry):
        pl.semaphore_signal(barrier, inc=1, device_id={"store": (me + i) % ns}, device_id_type=MESH)
        return carry

    def greet_grp(i, carry):
        pl.semaphore_signal(barrier, inc=1, device_id={"grp": (z + i) % nz}, device_id_type=MESH)
        return carry

    lax.fori_loop(far_lo, far_hi, greet_store, 0)
    lax.fori_loop(nz // 4, nz - nz // 4, greet_grp, 0)
    for low, high in near:
        lax.fori_loop(low, high, greet_store, 0)
    lax.fori_loop(1, nz // 4, greet_grp, 0)
    lax.fori_loop(nz - nz // 4, nz, greet_grp, 0)
    begin(3, 12)

    for i in range(3):
        settle("load", i)
    lane_s = lax.broadcasted_iota(I32, (ns, 128), 1)
    eye_o = lax.broadcasted_iota(I32, (ns, ns), 0) == lax.broadcasted_iota(I32, (ns, ns), 1)

    def column(row):
        spread = jnp.broadcast_to(row.astype(F32), (ns, ns))
        return jnp.sum(jnp.where(eye_o, spread, 0.0), axis=1, keepdims=True)

    count_row = bcnt_v[...]
    entries = [column(hid_v[c : c + 1, :]) for c in range(2)]
    entries += [column(jnp.where(count_row > c, bid_v[c : c + 1, :], nr)) for c in range(2)]
    message = entries[3]
    for c in (2, 1, 0):
        message = jnp.where(lane_s == c, entries[c], message)
    id_s[...] = message.astype(I32).reshape(ns, 1, 128)

    pl.semaphore_wait(barrier, ns - 1 + nz - 1)

    def arrive(buffer, count, sem):
        part = buffer.at[pl.ds(0, count)]
        pltpu.make_async_copy(part, part, sem).wait()

    def send_all(ranges, source, target, ssem, rsem, by_owner):
        def send(i, carry):
            along = i // w
            column = (my_w + i % w) % w
            peer = ((my_y + along) % ny) * w + column
            here = along * w + column
            there = ((ny - along) % ny) * w + my_w
            pltpu.make_async_remote_copy(
                src_ref=source.at[here if by_owner else peer],
                dst_ref=target.at[me if by_owner else there],
                send_sem=ssem,
                recv_sem=rsem,
                device_id={"store": peer},
                device_id_type=MESH,
            ).start()
            return carry

        for low, high in ranges:
            if low < high:
                lax.fori_loop(low, high, send, 0)
        return sum(high - low for low, high in ranges)

    def owe(name, buffer, count, sem):
        owed[name] = functools.partial(arrive, buffer, count, sem)

    def push(name, source, target, sems):
        count = send_all(far + near, source, target, sems.at[0], sems.at[1], False)
        owe((name, "out"), source, count, sems.at[0])
        owe((name, "in"), target, count, sems.at[1])

    for part, ranges in enumerate((far, near)):
        count = send_all(ranges, id_s, id_r, id_sem.at[part, 0], id_sem.at[part, 1], False)
        owe(("ids", "out", part), id_s, count, id_sem.at[part, 0])
        owe(("ids", "in", part), id_r, count, id_sem.at[part, 1])
    id_r[my_w] = id_s[me]

    for i in range(3, 6):
        settle("load", i)
    slot_row = lax.broadcasted_iota(I32, (nr, ns), 0)
    owner_lane = lax.broadcasted_iota(I32, (nr, ns), 1)
    of_owner = (slot_row >> 1) == owner_lane
    slot_c = (lax.broadcasted_iota(I32, (nr, 1), 0) & 1).astype(F32)

    def live(counts):
        spread = jnp.broadcast_to(counts[...].astype(F32), (nr, ns))
        count = jnp.sum(jnp.where(of_owner, spread, 0.0), axis=1, keepdims=True)
        return jnp.where(slot_c < count, 1.0, 0.0)

    live_b = live(bcnt_v)
    live_h = live(hcnt_v)

    blk = nr // 2
    for r in range(2):
        acc = jnp.zeros((blk, 4 * blk), F32)
        for k in range(4):
            lane = lax.broadcasted_iota(I32, (blk, 4 * blk), 1)
            row = lax.broadcasted_iota(I32, (blk, 4 * blk), 0)
            target = row + cols_v[r : r + 1, k : k + 1] * blk
            select = jnp.where(lane == target, 1.0, 0.0).astype(BF)
            acc += jnp.dot(vals_v[r, k], select, preferred_element_type=F32)
        adj[r * blk : (r + 1) * blk, :] = acc.astype(BF)

    def to_message(rows, stage, buffer):
        for b in range(cb):
            stage[pl.ds(b, nr, stride=cb), :] = rows[:, b * 128 : (b + 1) * 128].astype(F32)
        buffer[...] = stage[...].astype(BF).reshape(ns, 2 * cb, 128)

    settle("load", 6)
    rows1[0:nr, :] = (x_v[...].astype(F32) * live_b).astype(BF)
    to_message(rows1[0:nr, :], stage_a, push_s0)
    if PUSH0 == 3:
        push("push0", push_s0, push_r0, push_sem.at[0])
    push_r0[my_w] = push_s0[me]
    settle("load", 7)
    def hot(k, low, high):
        asked = id_r[low:high].reshape(high - low, 128)
        lane_r = lax.broadcasted_iota(I32, (high - low, nr), 1)
        return jnp.where(asked[:, k : k + 1] == lane_r, 1.0, 0.0)

    def gather(layer, ranges, stage, buffer):
        for low, high in ranges:
            size = high - low
            if size == 0:
                continue
            wanted = jnp.concatenate([hot(0, low, high), hot(1, low, high)], axis=0).astype(BF)
            found = jnp.dot(wanted, hist_v[layer], preferred_element_type=F32)
            for c in range(2):
                for b in range(cb):
                    stage[pl.ds(low * 2 * cb + c * cb + b, size, stride=2 * cb), :] = found[
                        c * size : (c + 1) * size, b * 128 : (b + 1) * 128
                    ]
            rows = stage[low * 2 * cb : high * 2 * cb, :]
            buffer[low:high] = rows.astype(BF).reshape(size, 2 * cb, 128)

    def reply(layer, ranges, source, target, sems, part):
        count = send_all(ranges, source, target, sems.at[part], sems.at[2], True)
        owe(("reply", layer, part), source, count, sems.at[part])

    near_rows = [(0, far_lo), (far_hi, ns)]
    settle("ids", "in", 1)
    gather(0, near_rows, stage_b, halo_s0)
    reply(0, near, halo_s0, halo_r0, halo_sem.at[0], 0)
    if NEAR1 == 1:
        gather(1, near_rows, stage_c, halo_s1)
        reply(1, near, halo_s1, halo_r1, halo_sem.at[1], 0)
    settle("ids", "in", 0)
    gather(0, far, stage_b, halo_s0)
    reply(0, far, halo_s0, halo_r0, halo_sem.at[0], 1)
    gather(1, far, stage_c, halo_s1)
    reply(1, far, halo_s1, halo_r1, halo_sem.at[1], 1)
    if NEAR1 == 0:
        gather(1, near_rows, stage_c, halo_s1)
        reply(1, near, halo_s1, halo_r1, halo_sem.at[1], 0)
    owe(("halo0", "in"), halo_r0, ns - 1, halo_sem.at[0, 2])
    owe(("halo1", "in"), halo_r1, ns - 1, halo_sem.at[1, 2])
    if PUSH0 == 0:
        push("push0", push_s0, push_r0, push_sem.at[0])
    halo_r0[me] = halo_s0[my_w]
    halo_r1[me] = halo_s1[my_w]

    def land(buffer, stage, rows):
        stage[...] = buffer[...].reshape(nr * cb, 128).astype(F32)
        for b in range(cb):
            block = stage[pl.ds(b, nr, stride=cb), :] * live_h
            rows[nr : 2 * nr, b * 128 : (b + 1) * 128] = block.astype(BF)

    def support(rows):
        for n in range(h // CW):
            part = slice(n * CW, (n + 1) * CW)
            aggregate = jnp.dot(adj[...], rows[:, part], preferred_element_type=F32)
            mixed = (1.0 - ALPHA) * aggregate + ALPHA * init_v[:, part].astype(F32)
            sup[:, part] = mixed.astype(BF)

    def preact(weight, beta, part):
        product = jnp.dot(sup[...], weight[:, part], preferred_element_type=F32)
        return (1.0 - beta) * sup[:, part].astype(F32) + beta * product

    settle("load", 8)
    settle("load", 9)
    settle("halo0", "in")
    land(halo_r0, stage_b, rows1)
    support(rows1)
    for n in range(h // CW):
        part = slice(n * CW, (n + 1) * CW)
        pre = preact(w1_v, BETA_ONE, part)
        inner = jnp.tanh(GELU_K * (pre + GELU_C * (pre * pre * pre)))
        fresh = (0.5 * pre * (1.0 + inner)).astype(BF).astype(F32)
        rows2[0:nr, part] = (fresh * live_b).astype(BF)
    to_message(rows2[0:nr, :], stage_a, push_s1)
    push("push1", push_s1, push_r1, push_sem.at[1])
    push_r1[my_w] = push_s1[me]
    if PUSH0 == 1:
        push("push0", push_s0, push_r0, push_sem.at[0])

    settle("load", 10)
    settle("load", 11)
    settle("halo1", "in")
    land(halo_r1, stage_c, rows2)
    support(rows2)

    wide = 4 * nx * j
    half = wide // 2
    lane_from = lax.broadcasted_iota(I32, (wide, wide), 1)
    row_to = lax.broadcasted_iota(I32, (wide, wide), 0)
    lg_j = j.bit_length() - 1
    lg_x = nx.bit_length() - 1
    from_j = lane_from & (j - 1)
    from_c = (lane_from >> lg_j) & 1
    from_x = (lane_from >> (lg_j + 1)) & (nx - 1)
    from_y = lane_from >> (lg_j + 1 + lg_x)
    goes = from_c * half + from_y * (nx * j) + from_x * j + from_j
    shuffle = jnp.where(goes == row_to, 1.0, 0.0).astype(BF)
    for t in range(h // wide):
        moved = lax.dot_general(
            shuffle,
            sup[:, t * wide : (t + 1) * wide],
            (((1,), (1,)), ((), ())),
            preferred_element_type=F32,
        ).astype(BF)
        sup_c[0, t * half : (t + 1) * half, :] = moved[:half]
        sup_c[1, t * half : (t + 1) * half, :] = moved[half:]
    partner = device(my_y, my_x, 1 - core)

    def to_partner(name, source, target, ssem, rsem):
        copy = pltpu.make_async_remote_copy(
            src_ref=source,
            dst_ref=target,
            send_sem=ssem,
            recv_sem=rsem,
            device_id=partner,
            device_id_type=MESH,
        )
        copy.start()
        owed[name] = copy.wait

    to_partner(("core", "s"), sup_c.at[1 - core], s_pair.at[1], core_sem.at[nch, 0], core_sem.at[nch, 1])
    s_pair[0] = sup_c[core]

    factor = BETA_TWO / math.sqrt(nz * ns * nr)

    along_x = (nx, my_x, lambda to: device(my_y, to, core))
    along_y = (ny, my_y, lambda to: device(to, my_x, core))

    def steps(count):
        if FAR_FIRST:
            return sorted(range(1, count), key=lambda i: -min(i, count - i))
        return range(1, count)

    def spread(name, k, axis, source, target, ssem, rsem):
        count, mine, to_device = axis
        for i in steps(count):
            to = (mine + i) % count
            pltpu.make_async_remote_copy(
                src_ref=source.at[to],
                dst_ref=target.at[i - 1],
                send_sem=ssem,
                recv_sem=rsem,
                device_id=to_device(to),
                device_id_type=MESH,
            ).start()
        owe((name, "in", k), target, count - 1, rsem)
        owe((name, "out", k), source, count - 1, ssem)

    def summed(axis, source, target):
        total = source[axis[1]].astype(F32)
        for i in range(axis[0] - 1):
            total += target[i].astype(F32)
        return total

    for n in range(nch + 1):
        if n < nch:
            part = slice(starts[n], starts[n] + WIDTHS[n])
            pre = preact(w2_v, BETA_TWO, part)
            square = pre * pre
            inner = jnp.tanh(GELU_K * (pre + GELU_C * (square * pre)))
            slope = 0.5 * (1.0 + inner) + 0.5 * pre * (1.0 - inner * inner) * (
                GELU_K * (1.0 + 3.0 * GELU_C * square)
            )
            g_pair[n][0] = (live_b * (cot_v[:, part].astype(F32) * slope)).astype(BF)
            to_partner(("core", n), g_pair[n].at[0], g_pair[n].at[1], core_sem.at[n, 0], core_sem.at[n, 1])
        if n == 1:
            settle("core", "s")
        if n >= 1:
            k = n - 1
            settle("core", k)
            share = factor * jnp.dot(
                jnp.concatenate([s_pair[0], s_pair[1]], axis=1),
                g_pair[k][...].reshape(2 * nr, WIDTHS[k]),
                preferred_element_type=F32,
            )
            if PATHS[k] == "x":
                for y in range(ny):
                    for x in range(nx):
                        at = (y * nx + x) * j
                        xs[k][x, y * j : (y + 1) * j, :] = share[at : at + j, :].astype(BF)
            else:
                xs[k][...] = share.astype(BF).reshape(ny, nx * j, WIDTHS[k])
            first = along_x if PATHS[k] == "x" else along_y
            spread("x", k, first, xs[k], xr[k], x_ssem.at[k], x_rsem.at[k])

    for k in range(nch + 1):
        if k < nch:
            first, second = (along_x, along_y) if PATHS[k] == "x" else (along_y, along_x)
            settle("x", "in", k)
            total = summed(first, xs[k], xr[k])
            ys[k][...] = total.astype(BF).reshape(second[0], j, WIDTHS[k])
            spread("y", k, second, ys[k], yr[k], y_ssem.at[k], y_rsem.at[k])
        if k >= 1:
            second = along_y if PATHS[k - 1] == "x" else along_x
            settle("y", "in", k - 1)
            total = summed(second, ys[k - 1], yr[k - 1])
            zr[k - 1][z] = total.astype(BF)
            for i in steps(nz):
                pltpu.make_async_remote_copy(
                    src_ref=zr[k - 1].at[z],
                    dst_ref=zr[k - 1].at[z],
                    send_sem=z_ssem.at[k - 1],
                    recv_sem=z_rsem.at[k - 1],
                    device_id={"grp": (z + i) % nz},
                    device_id_type=MESH,
                ).start()
            owed["z", "in", k - 1] = functools.partial(arrive, zr[k - 1], nz - 1, z_rsem.at[k - 1])
            owed["z", "out", k - 1] = functools.partial(arrive, zr[k - 1], nz - 1, z_ssem.at[k - 1])

    eye_r = lax.broadcasted_iota(I32, (nr, nr), 0) == lax.broadcasted_iota(I32, (nr, nr), 1)
    placed = jnp.concatenate([hot(2, 0, ns), hot(3, 0, ns)], axis=0)
    kept = jnp.where(eye_r, 1.0 - jnp.sum(placed, axis=0, keepdims=True), 0.0)
    place = jnp.concatenate([placed, kept], axis=0).astype(BF)

    def write_layer(layer, buffer, stage, rows):
        stage[...] = buffer[...].reshape(nr * cb, 128).astype(F32)
        for c in range(2):
            for b in range(cb):
                rows[c * ns : (c + 1) * ns, b * 128 : (b + 1) * 128] = stage[
                    pl.ds(c * cb + b, ns, stride=2 * cb), :
                ].astype(BF)
        rows[nr : 2 * nr, :] = hist_v[layer]
        hist_o[layer] = lax.dot_general(
            place, rows[...], (((0,), (0,)), ((), ())), preferred_element_type=F32
        ).astype(BF)
        store = pltpu.make_async_copy(hist_o.at[layer], newhist.at[layer, 0], osem.at[layer])
        store.start()
        owed["store", layer] = store.wait

    settle("push0", "in")
    write_layer(0, push_r0, stage_b, rows1)
    settle("push1", "in")
    write_layer(1, push_r1, stage_c, rows2)

    for k in range(nch):
        settle("z", "in", k)
        total = zr[k][0].astype(F32)
        for i in range(1, nz):
            total += zr[k][i].astype(F32)
        part = pl.ds(starts[k], WIDTHS[k])
        grad_v[:, part] = total
        store = pltpu.make_async_copy(grad_v.at[:, part], grad.at[:, part], osem.at[2 + k])
        store.start()
        owed["store", 2 + k] = store.wait
    finish()


def copy_kernel(a, b, a_out, b_out):
    a_out[...] = a[...]
    b_out[...] = b[...]


def per_device(*args):
    x, init, hist, bid, bcnt, hid, hcnt, cols, vals, w1, w2, cot = args
    ns, nz = lax.axis_size("store"), lax.axis_size("grp")
    h = x.shape[-1]
    nx = NX
    ny = ns // (2 * nx)
    j = h // ns
    nr = 2 * ns
    blk = nr // 2
    cb = h // 128
    nch = len(WIDTHS)
    vm = pltpu.VMEM
    dma = pltpu.SemaphoreType.DMA
    slots = vm((ns, 2 * cb, 128), BF)
    stage = vm((nr * cb, 128), F32)
    scratch = [
        vm((nr, h), BF),
        vm((nr, h), BF),
        vm((2, nr, h), BF),
        vm((2, ns), I32),
        vm((1, ns), I32),
        vm((2, ns), I32),
        vm((1, ns), I32),
        vm((2, 4), I32),
        vm((2, 4, blk, blk), BF),
        vm((h, h), BF),
        vm((h, h), BF),
        vm((nr, h), BF),
        vm((ns, 1, 128), I32),
        vm((ns, 1, 128), I32),
        stage,
        stage,
        stage,
        slots,
        slots,
        slots,
        slots,
        slots,
        slots,
        slots,
        slots,
        vm((nr, 2 * nr), BF),
        vm((2 * nr, h), BF),
        vm((2 * nr, h), BF),
        vm((nr, h), BF),
        vm((2, h // 2, nr), BF),
        vm((2, h // 2, nr), BF),
        vm((2, nr, h), BF),
        vm((j, h), F32),
        dma((12,)),
        dma((2, 2)),
        dma((2, 3)),
        dma((2, 2)),
        dma((nch + 1, 2)),
        dma((nch,)),
        dma((nch,)),
        dma((nch,)),
        dma((nch,)),
        dma((nch,)),
        dma((nch,)),
        dma((2 + nch,)),
    ]
    scratch += [vm((2, nr, c), BF) for c in WIDTHS]
    sizes = [(nx, ny, c) if p == "x" else (ny, nx, c) for p, c in zip(PATHS, WIDTHS)]
    scratch += [vm((a, b * j, c), BF) for a, b, c in sizes]
    scratch += [vm((a - 1, b * j, c), BF) for a, b, c in sizes]
    scratch += [vm((b, j, c), BF) for a, b, c in sizes]
    scratch += [vm((b - 1, j, c), BF) for a, b, c in sizes]
    scratch += [vm((nz, j, c), BF) for c in WIDTHS]
    results = pl.pallas_call(
        functools.partial(kernel, (ns, nz, ny, nx, h, j)),
        out_shape=(
            jax.ShapeDtypeStruct((2, 1, nr, h), BF),
            jax.ShapeDtypeStruct((j, h), F32),
        ),
        in_specs=[pl.BlockSpec(memory_space=pl.ANY)] * 12,
        out_specs=(
            pl.BlockSpec(memory_space=pl.ANY),
            pl.BlockSpec(memory_space=pl.ANY),
        ),
        scratch_shapes=scratch,
        compiler_params=pltpu.CompilerParams(
            collective_id=0, has_side_effects=True, vmem_limit_bytes=VMEM_BYTES
        ),
        name="gcnii",
    )(
        x,
        init,
        hist,
        jnp.swapaxes(bid, 2, 3),
        bcnt,
        jnp.swapaxes(hid, 2, 3),
        hcnt,
        cols,
        vals,
        w1,
        w2,
        cot,
    )
    specs = (
        pl.BlockSpec((2, 1, nr // 2, h), lambda i: (0, 0, i, 0)),
        pl.BlockSpec((j, h // 2), lambda i: (0, i)),
    )
    return pl.pallas_call(
        copy_kernel,
        grid=(2,),
        out_shape=(
            jax.ShapeDtypeStruct((2, 1, nr, h), BF),
            jax.ShapeDtypeStruct((j, h), F32),
        ),
        in_specs=specs,
        out_specs=specs,
        compiler_params=pltpu.CompilerParams(vmem_limit_bytes=VMEM_BYTES),
        name="write_out",
    )(*results)


def solution(mesh):
    in_specs = (
        P("grp", "store", None, None),
        P("grp", "store", None, None),
        P(None, "grp", "store", None),
        P("grp", "store", None, None),
        P("grp", "store", None),
        P("grp", "store", None, None),
        P("grp", "store", None),
        P("grp", "store", None, None),
        P("grp", "store", None, None, None, None),
        P(),
        P(),
        P("grp", "store", None, None),
    )
    out_specs = (P(None, "grp", "store", None), P("store", None))
    return jax.shard_map(
        per_device, mesh=mesh, in_specs=in_specs, out_specs=out_specs, check_vma=False
    )
```

```python
import functools
import math

import jax
import jax.numpy as jnp
from jax import lax
from jax.experimental import pallas as pl
from jax.experimental.pallas import tpu as pltpu
from jax.sharding import PartitionSpec as P

ALPHA = 0.1
BETA_ONE = math.log(1.5)
BETA_TWO = math.log(1.25)
GELU_K = math.sqrt(2.0 / math.pi)
GELU_C = 0.044715
MESH = pl.DeviceIdType.MESH
NX = 4
WIDTHS = (256, 384, 256, 128)
PATHS = "xxxx"
FAR_FIRST = 1
CW = 256
FAR = {8: (3, 6), 2: (1, 2)}
PUSH0 = 3
NEAR1 = 0
VMEM_BYTES = 63 << 20
F32 = jnp.float32
BF = jnp.bfloat16
I32 = jnp.int32


def kernel(
    dims,
    x_hbm,
    init_hbm,
    hist_hbm,
    bid_hbm,
    bcnt_hbm,
    hid_hbm,
    hcnt_hbm,
    cols_hbm,
    vals_hbm,
    w1_hbm,
    w2_hbm,
    cot_hbm,
    newhist,
    grad,
    x_v,
    init_v,
    hist_v,
    bid_v,
    bcnt_v,
    hid_v,
    hcnt_v,
    cols_v,
    vals_v,
    w1_v,
    w2_v,
    cot_v,
    id_s,
    id_r,
    stage_a,
    stage_b,
    stage_c,
    halo_s0,
    halo_s1,
    halo_r0,
    halo_r1,
    push_s0,
    push_s1,
    push_r0,
    push_r1,
    adj,
    rows1,
    rows2,
    sup,
    sup_c,
    s_pair,
    hist_o,
    grad_v,
    lsem,
    id_sem,
    halo_sem,
    push_sem,
    core_sem,
    x_ssem,
    x_rsem,
    y_ssem,
    y_rsem,
    z_ssem,
    z_rsem,
    osem,
    *chunks,
):
    ns, nz, ny, nx, h, j = dims
    cb = h // 128
    nr = 2 * ns
    nch = len(WIDTHS)
    starts = [sum(WIDTHS[:k]) for k in range(nch)]
    g_pair, xs, xr, ys, yr, zr = (chunks[i * nch : (i + 1) * nch] for i in range(6))
    w = 2 * nx
    far_lo, far_hi = (d * w for d in FAR[ny])
    near = [(1, far_lo), (far_hi, ns)]
    far = [(far_lo, far_hi)]
    me = lax.axis_index("store")
    z = lax.axis_index("grp")
    core = me % 2
    my_x = (me // 2) % nx
    my_y = me // w
    my_w = me % w

    def device(y, x, c):
        return {"store": (y * nx + x) * 2 + c}

    locals_ = [
        (hid_hbm.at[0, 0], hid_v),
        (bid_hbm.at[0, 0], bid_v),
        (bcnt_hbm.at[0], bcnt_v),
        (hcnt_hbm.at[0], hcnt_v),
        (cols_hbm.at[0, 0], cols_v),
        (vals_hbm.at[0, 0], vals_v),
        (x_hbm.at[0, 0], x_v),
        (hist_hbm.at[:, 0], hist_v),
        (init_hbm.at[0, 0], init_v),
        (w1_hbm, w1_v),
        (w2_hbm, w2_v),
        (cot_hbm.at[0, 0], cot_v),
    ]
    loads = [pltpu.make_async_copy(a, b, lsem.at[i]) for i, (a, b) in enumerate(locals_)]
    owed = {}

    def begin(first, last):
        for i in range(first, last):
            loads[i].start()
            owed["load", i] = loads[i].wait

    begin(0, 3)

    def settle(*name):
        owed.pop(name)()

    def finish():
        for name in list(owed):
            owed.pop(name)()

    barrier = pltpu.get_barrier_semaphore()

    def greet_store(i, carry):
        pl.semaphore_signal(barrier, inc=1, device_id={"store": (me + i) % ns}, device_id_type=MESH)
        return carry

    def greet_grp(i, carry):
        pl.semaphore_signal(barrier, inc=1, device_id={"grp": (z + i) % nz}, device_id_type=MESH)
        return carry

    lax.fori_loop(far_lo, far_hi, greet_store, 0)
    lax.fori_loop(nz // 4, nz - nz // 4, greet_grp, 0)
    for low, high in near:
        lax.fori_loop(low, high, greet_store, 0)
    lax.fori_loop(1, nz // 4, greet_grp, 0)
    lax.fori_loop(nz - nz // 4, nz, greet_grp, 0)
    begin(3, 12)

    for i in range(3):
        settle("load", i)
    lane_s = lax.broadcasted_iota(I32, (ns, 128), 1)
    eye_o = lax.broadcasted_iota(I32, (ns, ns), 0) == lax.broadcasted_iota(I32, (ns, ns), 1)

    def column(row):
        spread = jnp.broadcast_to(row.astype(F32), (ns, ns))
        return jnp.sum(jnp.where(eye_o, spread, 0.0), axis=1, keepdims=True)

    count_row = bcnt_v[...]
    entries = [column(hid_v[c : c + 1, :]) for c in range(2)]
    entries += [column(jnp.where(count_row > c, bid_v[c : c + 1, :], nr)) for c in range(2)]
    message = entries[3]
    for c in (2, 1, 0):
        message = jnp.where(lane_s == c, entries[c], message)
    id_s[...] = message.astype(I32).reshape(ns, 1, 128)

    pl.semaphore_wait(barrier, ns - 1 + nz - 1)

    def arrive(buffer, count, sem):
        part = buffer.at[pl.ds(0, count)]
        pltpu.make_async_copy(part, part, sem).wait()

    def send_all(ranges, source, target, ssem, rsem, by_owner):
        def send(i, carry):
            along = i // w
            column = (my_w + i % w) % w
            peer = ((my_y + along) % ny) * w + column
            here = along * w + column
            there = ((ny - along) % ny) * w + my_w
            pltpu.make_async_remote_copy(
                src_ref=source.at[here if by_owner else peer],
                dst_ref=target.at[me if by_owner else there],
                send_sem=ssem,
                recv_sem=rsem,
                device_id={"store": peer},
                device_id_type=MESH,
            ).start()
            return carry

        for low, high in ranges:
            if low < high:
                lax.fori_loop(low, high, send, 0)
        return sum(high - low for low, high in ranges)

    def owe(name, buffer, count, sem):
        owed[name] = functools.partial(arrive, buffer, count, sem)

    def push(name, source, target, sems):
        count = send_all(far + near, source, target, sems.at[0], sems.at[1], False)
        owe((name, "out"), source, count, sems.at[0])
        owe((name, "in"), target, count, sems.at[1])

    for part, ranges in enumerate((far, near)):
        count = send_all(ranges, id_s, id_r, id_sem.at[part, 0], id_sem.at[part, 1], False)
        owe(("ids", "out", part), id_s, count, id_sem.at[part, 0])
        owe(("ids", "in", part), id_r, count, id_sem.at[part, 1])
    id_r[my_w] = id_s[me]

    for i in range(3, 6):
        settle("load", i)
    slot_row = lax.broadcasted_iota(I32, (nr, ns), 0)
    owner_lane = lax.broadcasted_iota(I32, (nr, ns), 1)
    of_owner = (slot_row >> 1) == owner_lane
    slot_c = (lax.broadcasted_iota(I32, (nr, 1), 0) & 1).astype(F32)

    def live(counts):
        spread = jnp.broadcast_to(counts[...].astype(F32), (nr, ns))
        count = jnp.sum(jnp.where(of_owner, spread, 0.0), axis=1, keepdims=True)
        return jnp.where(slot_c < count, 1.0, 0.0)

    live_b = live(bcnt_v)
    live_h = live(hcnt_v)

    blk = nr // 2
    for r in range(2):
        acc = jnp.zeros((blk, 4 * blk), F32)
        for k in range(4):
            lane = lax.broadcasted_iota(I32, (blk, 4 * blk), 1)
            row = lax.broadcasted_iota(I32, (blk, 4 * blk), 0)
            target = row + cols_v[r : r + 1, k : k + 1] * blk
            select = jnp.where(lane == target, 1.0, 0.0).astype(BF)
            acc += jnp.dot(vals_v[r, k], select, preferred_element_type=F32)
        adj[r * blk : (r + 1) * blk, :] = acc.astype(BF)

    def to_message(rows, stage, buffer):
        for b in range(cb):
            stage[pl.ds(b, nr, stride=cb), :] = rows[:, b * 128 : (b + 1) * 128].astype(F32)
        buffer[...] = stage[...].astype(BF).reshape(ns, 2 * cb, 128)

    settle("load", 6)
    rows1[0:nr, :] = (x_v[...].astype(F32) * live_b).astype(BF)
    to_message(rows1[0:nr, :], stage_a, push_s0)
    if PUSH0 == 3:
        push("push0", push_s0, push_r0, push_sem.at[0])
    push_r0[my_w] = push_s0[me]
    settle("load", 7)
    def hot(k, low, high):
        asked = id_r[low:high].reshape(high - low, 128)
        lane_r = lax.broadcasted_iota(I32, (high - low, nr), 1)
        return jnp.where(asked[:, k : k + 1] == lane_r, 1.0, 0.0)

    def gather(layer, ranges, stage, buffer):
        for low, high in ranges:
            size = high - low
            if size == 0:
                continue
            wanted = jnp.concatenate([hot(0, low, high), hot(1, low, high)], axis=0).astype(BF)
            found = jnp.dot(wanted, hist_v[layer], preferred_element_type=F32)
            for c in range(2):
                for b in range(cb):
                    stage[pl.ds(low * 2 * cb + c * cb + b, size, stride=2 * cb), :] = found[
                        c * size : (c + 1) * size, b * 128 : (b + 1) * 128
                    ]
            rows = stage[low * 2 * cb : high * 2 * cb, :]
            buffer[low:high] = rows.astype(BF).reshape(size, 2 * cb, 128)

    def reply(layer, ranges, source, target, sems, part):
        count = send_all(ranges, source, target, sems.at[part], sems.at[2], True)
        owe(("reply", layer, part), source, count, sems.at[part])

    near_rows = [(0, far_lo), (far_hi, ns)]
    settle("ids", "in", 1)
    gather(0, near_rows, stage_b, halo_s0)
    reply(0, near, halo_s0, halo_r0, halo_sem.at[0], 0)
    if NEAR1 == 1:
        gather(1, near_rows, stage_c, halo_s1)
        reply(1, near, halo_s1, halo_r1, halo_sem.at[1], 0)
    settle("ids", "in", 0)
    gather(0, far, stage_b, halo_s0)
    reply(0, far, halo_s0, halo_r0, halo_sem.at[0], 1)
    gather(1, far, stage_c, halo_s1)
    reply(1, far, halo_s1, halo_r1, halo_sem.at[1], 1)
    if NEAR1 == 0:
        gather(1, near_rows, stage_c, halo_s1)
        reply(1, near, halo_s1, halo_r1, halo_sem.at[1], 0)
    owe(("halo0", "in"), halo_r0, ns - 1, halo_sem.at[0, 2])
    owe(("halo1", "in"), halo_r1, ns - 1, halo_sem.at[1, 2])
    if PUSH0 == 0:
        push("push0", push_s0, push_r0, push_sem.at[0])
    halo_r0[me] = halo_s0[my_w]
    halo_r1[me] = halo_s1[my_w]

    def land(buffer, stage, rows):
        stage[...] = buffer[...].reshape(nr * cb, 128).astype(F32)
        for b in range(cb):
            block = stage[pl.ds(b, nr, stride=cb), :] * live_h
            rows[nr : 2 * nr, b * 128 : (b + 1) * 128] = block.astype(BF)

    def support(rows):
        for n in range(h // CW):
            part = slice(n * CW, (n + 1) * CW)
            aggregate = jnp.dot(adj[...], rows[:, part], preferred_element_type=F32)
            mixed = (1.0 - ALPHA) * aggregate + ALPHA * init_v[:, part].astype(F32)
            sup[:, part] = mixed.astype(BF)

    def preact(weight, beta, part):
        product = jnp.dot(sup[...], weight[:, part], preferred_element_type=F32)
        return (1.0 - beta) * sup[:, part].astype(F32) + beta * product

    settle("load", 8)
    settle("load", 9)
    settle("halo0", "in")
    land(halo_r0, stage_b, rows1)
    support(rows1)
    for n in range(h // CW):
        part = slice(n * CW, (n + 1) * CW)
        pre = preact(w1_v, BETA_ONE, part)
        inner = jnp.tanh(GELU_K * (pre + GELU_C * (pre * pre * pre)))
        fresh = (0.5 * pre * (1.0 + inner)).astype(BF).astype(F32)
        rows2[0:nr, part] = (fresh * live_b).astype(BF)
    to_message(rows2[0:nr, :], stage_a, push_s1)
    push("push1", push_s1, push_r1, push_sem.at[1])
    push_r1[my_w] = push_s1[me]
    if PUSH0 == 1:
        push("push0", push_s0, push_r0, push_sem.at[0])

    settle("load", 10)
    settle("load", 11)
    settle("halo1", "in")
    land(halo_r1, stage_c, rows2)
    support(rows2)

    wide = 4 * nx * j
    half = wide // 2
    lane_from = lax.broadcasted_iota(I32, (wide, wide), 1)
    row_to = lax.broadcasted_iota(I32, (wide, wide), 0)
    lg_j = j.bit_length() - 1
    lg_x = nx.bit_length() - 1
    from_j = lane_from & (j - 1)
    from_c = (lane_from >> lg_j) & 1
    from_x = (lane_from >> (lg_j + 1)) & (nx - 1)
    from_y = lane_from >> (lg_j + 1 + lg_x)
    goes = from_c * half + from_y * (nx * j) + from_x * j + from_j
    shuffle = jnp.where(goes == row_to, 1.0, 0.0).astype(BF)
    for t in range(h // wide):
        moved = lax.dot_general(
            shuffle,
            sup[:, t * wide : (t + 1) * wide],
            (((1,), (1,)), ((), ())),
            preferred_element_type=F32,
        ).astype(BF)
        sup_c[0, t * half : (t + 1) * half, :] = moved[:half]
        sup_c[1, t * half : (t + 1) * half, :] = moved[half:]
    partner = device(my_y, my_x, 1 - core)

    def to_partner(name, source, target, ssem, rsem):
        copy = pltpu.make_async_remote_copy(
            src_ref=source,
            dst_ref=target,
            send_sem=ssem,
            recv_sem=rsem,
            device_id=partner,
            device_id_type=MESH,
        )
        copy.start()
        owed[name] = copy.wait

    to_partner(("core", "s"), sup_c.at[1 - core], s_pair.at[1], core_sem.at[nch, 0], core_sem.at[nch, 1])
    s_pair[0] = sup_c[core]

    factor = BETA_TWO / math.sqrt(nz * ns * nr)

    along_x = (nx, my_x, lambda to: device(my_y, to, core))
    along_y = (ny, my_y, lambda to: device(to, my_x, core))

    def steps(count):
        if FAR_FIRST:
            return sorted(range(1, count), key=lambda i: -min(i, count - i))
        return range(1, count)

    def spread(name, k, axis, source, target, ssem, rsem):
        count, mine, to_device = axis
        for i in steps(count):
            to = (mine + i) % count
            pltpu.make_async_remote_copy(
                src_ref=source.at[to],
                dst_ref=target.at[i - 1],
                send_sem=ssem,
                recv_sem=rsem,
                device_id=to_device(to),
                device_id_type=MESH,
            ).start()
        owe((name, "in", k), target, count - 1, rsem)
        owe((name, "out", k), source, count - 1, ssem)

    def summed(axis, source, target):
        total = source[axis[1]].astype(F32)
        for i in range(axis[0] - 1):
            total += target[i].astype(F32)
        return total

    for n in range(nch + 1):
        if n < nch:
            part = slice(starts[n], starts[n] + WIDTHS[n])
            pre = preact(w2_v, BETA_TWO, part)
            square = pre * pre
            inner = jnp.tanh(GELU_K * (pre + GELU_C * (square * pre)))
            slope = 0.5 * (1.0 + inner) + 0.5 * pre * (1.0 - inner * inner) * (
                GELU_K * (1.0 + 3.0 * GELU_C * square)
            )
            g_pair[n][0] = (live_b * (cot_v[:, part].astype(F32) * slope)).astype(BF)
            to_partner(("core", n), g_pair[n].at[0], g_pair[n].at[1], core_sem.at[n, 0], core_sem.at[n, 1])
        if n == 1:
            settle("core", "s")
        if n >= 1:
            k = n - 1
            settle("core", k)
            share = factor * jnp.dot(
                jnp.concatenate([s_pair[0], s_pair[1]], axis=1),
                g_pair[k][...].reshape(2 * nr, WIDTHS[k]),
                preferred_element_type=F32,
            )
            if PATHS[k] == "x":
                for y in range(ny):
                    for x in range(nx):
                        at = (y * nx + x) * j
                        xs[k][x, y * j : (y + 1) * j, :] = share[at : at + j, :].astype(BF)
            else:
                xs[k][...] = share.astype(BF).reshape(ny, nx * j, WIDTHS[k])
            first = along_x if PATHS[k] == "x" else along_y
            spread("x", k, first, xs[k], xr[k], x_ssem.at[k], x_rsem.at[k])

    for k in range(nch + 1):
        if k < nch:
            first, second = (along_x, along_y) if PATHS[k] == "x" else (along_y, along_x)
            settle("x", "in", k)
            total = summed(first, xs[k], xr[k])
            ys[k][...] = total.astype(BF).reshape(second[0], j, WIDTHS[k])
            spread("y", k, second, ys[k], yr[k], y_ssem.at[k], y_rsem.at[k])
        if k >= 1:
            second = along_y if PATHS[k - 1] == "x" else along_x
            settle("y", "in", k - 1)
            total = summed(second, ys[k - 1], yr[k - 1])
            zr[k - 1][z] = total.astype(BF)
            for i in steps(nz):
                pltpu.make_async_remote_copy(
                    src_ref=zr[k - 1].at[z],
                    dst_ref=zr[k - 1].at[z],
                    send_sem=z_ssem.at[k - 1],
                    recv_sem=z_rsem.at[k - 1],
                    device_id={"grp": (z + i) % nz},
                    device_id_type=MESH,
                ).start()
            owed["z", "in", k - 1] = functools.partial(arrive, zr[k - 1], nz - 1, z_rsem.at[k - 1])
            owed["z", "out", k - 1] = functools.partial(arrive, zr[k - 1], nz - 1, z_ssem.at[k - 1])

    eye_r = lax.broadcasted_iota(I32, (nr, nr), 0) == lax.broadcasted_iota(I32, (nr, nr), 1)
    placed = jnp.concatenate([hot(2, 0, ns), hot(3, 0, ns)], axis=0)
    kept = jnp.where(eye_r, 1.0 - jnp.sum(placed, axis=0, keepdims=True), 0.0)
    place = jnp.concatenate([placed, kept], axis=0).astype(BF)

    def write_layer(layer, buffer, stage, rows):
        stage[...] = buffer[...].reshape(nr * cb, 128).astype(F32)
        for c in range(2):
            for b in range(cb):
                rows[c * ns : (c + 1) * ns, b * 128 : (b + 1) * 128] = stage[
                    pl.ds(c * cb + b, ns, stride=2 * cb), :
                ].astype(BF)
        rows[nr : 2 * nr, :] = hist_v[layer]
        hist_o[layer] = lax.dot_general(
            place, rows[...], (((0,), (0,)), ((), ())), preferred_element_type=F32
        ).astype(BF)
        store = pltpu.make_async_copy(hist_o.at[layer], newhist.at[layer, 0], osem.at[layer])
        store.start()
        owed["store", layer] = store.wait

    settle("push0", "in")
    write_layer(0, push_r0, stage_b, rows1)
    settle("push1", "in")
    write_layer(1, push_r1, stage_c, rows2)

    for k in range(nch):
        settle("z", "in", k)
        total = zr[k][0].astype(F32)
        for i in range(1, nz):
            total += zr[k][i].astype(F32)
        part = pl.ds(starts[k], WIDTHS[k])
        grad_v[:, part] = total
        store = pltpu.make_async_copy(grad_v.at[:, part], grad.at[:, part], osem.at[2 + k])
        store.start()
        owed["store", 2 + k] = store.wait
    finish()


def copy_kernel(a, b, a_out, b_out):
    a_out[...] = a[...]
    b_out[...] = b[...]


def per_device(*args):
    x, init, hist, bid, bcnt, hid, hcnt, cols, vals, w1, w2, cot = args
    ns, nz = lax.axis_size("store"), lax.axis_size("grp")
    h = x.shape[-1]
    nx = NX
    ny = ns // (2 * nx)
    j = h // ns
    nr = 2 * ns
    blk = nr // 2
    cb = h // 128
    nch = len(WIDTHS)
    vm = pltpu.VMEM
    dma = pltpu.SemaphoreType.DMA
    slots = vm((ns, 2 * cb, 128), BF)
    stage = vm((nr * cb, 128), F32)
    scratch = [
        vm((nr, h), BF),
        vm((nr, h), BF),
        vm((2, nr, h), BF),
        vm((2, ns), I32),
        vm((1, ns), I32),
        vm((2, ns), I32),
        vm((1, ns), I32),
        vm((2, 4), I32),
        vm((2, 4, blk, blk), BF),
        vm((h, h), BF),
        vm((h, h), BF),
        vm((nr, h), BF),
        vm((ns, 1, 128), I32),
        vm((ns, 1, 128), I32),
        stage,
        stage,
        stage,
        slots,
        slots,
        slots,
        slots,
        slots,
        slots,
        slots,
        slots,
        vm((nr, 2 * nr), BF),
        vm((2 * nr, h), BF),
        vm((2 * nr, h), BF),
        vm((nr, h), BF),
        vm((2, h // 2, nr), BF),
        vm((2, h // 2, nr), BF),
        vm((2, nr, h), BF),
        vm((j, h), F32),
        dma((12,)),
        dma((2, 2)),
        dma((2, 3)),
        dma((2, 2)),
        dma((nch + 1, 2)),
        dma((nch,)),
        dma((nch,)),
        dma((nch,)),
        dma((nch,)),
        dma((nch,)),
        dma((nch,)),
        dma((2 + nch,)),
    ]
    scratch += [vm((2, nr, c), BF) for c in WIDTHS]
    sizes = [(nx, ny, c) if p == "x" else (ny, nx, c) for p, c in zip(PATHS, WIDTHS)]
    scratch += [vm((a, b * j, c), BF) for a, b, c in sizes]
    scratch += [vm((a - 1, b * j, c), BF) for a, b, c in sizes]
    scratch += [vm((b, j, c), BF) for a, b, c in sizes]
    scratch += [vm((b - 1, j, c), BF) for a, b, c in sizes]
    scratch += [vm((nz, j, c), BF) for c in WIDTHS]
    results = pl.pallas_call(
        functools.partial(kernel, (ns, nz, ny, nx, h, j)),
        out_shape=(
            jax.ShapeDtypeStruct((2, 1, nr, h), BF),
            jax.ShapeDtypeStruct((j, h), F32),
        ),
        in_specs=[pl.BlockSpec(memory_space=pl.ANY)] * 12,
        out_specs=(
            pl.BlockSpec(memory_space=pl.ANY),
            pl.BlockSpec(memory_space=pl.ANY),
        ),
        scratch_shapes=scratch,
        compiler_params=pltpu.CompilerParams(
            collective_id=0, has_side_effects=True, vmem_limit_bytes=VMEM_BYTES
        ),
        name="gcnii",
    )(
        x,
        init,
        hist,
        jnp.swapaxes(bid, 2, 3),
        bcnt,
        jnp.swapaxes(hid, 2, 3),
        hcnt,
        cols,
        vals,
        w1,
        w2,
        cot,
    )
    specs = (
        pl.BlockSpec((2, 1, nr // 2, h), lambda i: (0, 0, i, 0)),
        pl.BlockSpec((j, h // 2), lambda i: (0, i)),
    )
    return pl.pallas_call(
        copy_kernel,
        grid=(2,),
        out_shape=(
            jax.ShapeDtypeStruct((2, 1, nr, h), BF),
            jax.ShapeDtypeStruct((j, h), F32),
        ),
        in_specs=specs,
        out_specs=specs,
        compiler_params=pltpu.CompilerParams(vmem_limit_bytes=VMEM_BYTES),
        name="write_out",
    )(*results)


def solution(mesh):
    in_specs = (
        P("grp", "store", None, None),
        P("grp", "store", None, None),
        P(None, "grp", "store", None),
        P("grp", "store", None, None),
        P("grp", "store", None),
        P("grp", "store", None, None),
        P("grp", "store", None),
        P("grp", "store", None, None),
        P("grp", "store", None, None, None, None),
        P(),
        P(),
        P("grp", "store", None, None),
    )
    out_specs = (P(None, "grp", "store", None), P("store", None))
    return jax.shard_map(
        per_device, mesh=mesh, in_specs=in_specs, out_specs=out_specs, check_vma=False
    )
```
